32 devices in a mesh: tx: 4 (over x, core), gz: 8 (over z, y).
Axes of the slice: x: 2, y: 2, z: 4, core: 2. Of those that a mesh axis runs over, the one named last changes fastest.
Arguments:
- sources: float32 [4, 2, 128, 128, 128], P('tx', None, 'gz'), may hold values from -2 to 2
- contrast: float32 [2, 128, 128, 128], P(None, 'gz'), may hold values from -3 to 3
- spectrum: float32 [2, 256, 256, 256], P(None, None, 'gz'), may hold values from -6 to 6
- measured: float32 [4, 2, 1024], P('tx'), may hold values from -6.1 to 6.1
- receivers: int32 [4, 1024], P('tx'), may hold values from 0 to 2097151
- positions: int32 [4, 2], P('tx'), may hold values from 0 to 127
Outputs:
- sources_new: float32 [4, 2, 128, 128, 128], P('tx', None, 'gz')
- contrast_new: float32 [2, 128, 128, 128], P(None, 'gz')
The draws below stay inside these ranges and needn't reach their ends.
All inputs are finite; a program needn't handle non-finite values.
Results may differ from the reference program's by a relative error of at most 0.0001.
Values sent between devices are 32-bit elements; how exact they have to be, the bound alone decides.
No kernel may reach another device: no remote copies, remote signals or barrier semaphores. Data moves between devices by JAX's collectives and lax.ppermute only.
A program may use at most 768 MiB of HBM per device.

```python
import math
import jax
import jax.numpy as jnp
from jax import lax

NC = 128
NP = 256
TX = 4
NREC = 1024


def draw_measured(key, part):
    ramp = jnp.arange(TX, dtype=jnp.float32) / max(TX - 1, 1)
    values = jnp.clip(jax.random.normal(key, (TX, 2, NREC), jnp.float32), -5.0, 5.0)
    scales = 0.7 * jnp.exp(ramp * (0.5 * math.log(3.0)))
    return values * scales[:, None, None]


def touch_ends(values, rng, low, high):
    shape = values.shape
    spot = [jax.random.randint(jax.random.fold_in(rng, axis), (), 0, shape[axis]) for axis in range(len(shape))]
    values = values.at[tuple(spot)].set(low)
    longest = shape.index(max(shape))
    spot[longest] = (spot[longest] + 1) % shape[longest]
    return values.at[tuple(spot)].set(high)


def level_of(own_key, extent, pieces, smallest, high):
    level = 1.0
    for dim, parts in pieces:
        steps = jax.random.uniform(jax.random.fold_in(jax.random.fold_in(own_key, 6), dim), (parts,), jnp.float32, smallest / len(pieces), high / len(pieces))
        level = level * jnp.repeat(jnp.exp(steps), extent[dim] // parts).reshape((-1,) + (1,) * (len(extent) - 1 - dim))
    return level


def bell_draw(stream_key, shape, width, reach, cuts=(), kind=jnp.bfloat16):
    level = level_of(stream_key, shape, cuts, -0.22, 0.18) if cuts else 1.0
    array = jax.random.normal(stream_key, shape, jnp.float32) * width * level
    return jnp.minimum(jnp.maximum(array, -reach), reach).astype(kind)


def setup_inputs(seed: int = 0) -> dict:
    splits = jax.random.split(jax.random.key(seed), 7)
    return {
        "sources": bell_draw(splits[0], (TX, 2, NC, NC, NC), 0.3, 2.0, ((0, 4), (2, 8)), jnp.float32),
        "contrast": bell_draw(splits[1], (2, NC, NC, NC), 0.5, 3.0, ((1, 8),), jnp.float32),
        "spectrum": bell_draw(splits[2], (2, NP, NP, NP), 1.0, 6.0, ((2, 8),), jnp.float32),
        "measured": draw_measured(jax.random.fold_in(splits[6], 71), 0),
        "receivers": touch_ends(jax.random.randint(splits[4], (TX, NREC), 0, NC * NC * NC), jax.random.fold_in(splits[4], 1), 0, (NC * NC * NC) - 1).astype(jnp.int32),
        "positions": touch_ends(jax.random.randint(splits[5], (TX, 2), 0, NC), jax.random.fold_in(splits[5], 1), 0, NC - 1).astype(jnp.int32),
    }


wave_number = 2.0 * math.pi / 12.0
reach_cells = 16.0
tikhonov = 1.0
step_length = 0.5
norm_floor = 1e-06

def incident(position):
    grid_shape = (NC, NC, NC)
    first_axis = lax.broadcasted_iota(jnp.int32, grid_shape, 0) + NC // 4
    along_second = lax.broadcasted_iota(jnp.int32, grid_shape, 1) - position[0]
    along_third = lax.broadcasted_iota(jnp.int32, grid_shape, 2) - position[1]
    squared = first_axis * first_axis + along_second * along_second + along_third * along_third
    radius = jnp.sqrt(squared.astype(jnp.float32))
    amplitude = reach_cells / (reach_cells + radius)
    return (amplitude * jnp.cos(wave_number * radius), amplitude * jnp.sin(wave_number * radius))

def convolve(real_part, imag_part, spec_real, spec_imag):
    complex_field = lax.complex(real_part, imag_part)
    padded = jnp.pad(complex_field, ((0, NC), (0, NC), (0, NC)))
    spectral = jnp.fft.fftn(padded) * lax.complex(spec_real, spec_imag)
    result = jnp.fft.ifftn(spectral)[:NC, :NC, :NC]
    return (jnp.real(result), jnp.imag(result))

def reference(sources, contrast, spectrum, measured, receivers, positions):
    zeros = jnp.zeros((NC, NC, NC), jnp.float32)

    def forward_step(running, step_items):
        source, position = step_items
        inc_real, inc_imag = incident(position)
        scat_real, scat_imag = convolve(source[0], source[1], spectrum[0], spectrum[1])
        total_real = inc_real + scat_real
        total_imag = inc_imag + scat_imag
        numer_real = running[0] + (source[0] * total_real + source[1] * total_imag)
        numer_imag = running[1] + (source[1] * total_real - source[0] * total_imag)
        weight = running[2] + (total_real * total_real + total_imag * total_imag)
        return ((numer_real, numer_imag, weight), jnp.stack([scat_real, scat_imag]))
    sums, scattered = lax.scan(forward_step, (zeros, zeros, zeros), (sources, positions))
    numer_real, numer_imag, weight = sums
    chi_real = (numer_real + tikhonov * contrast[0]) / (weight + tikhonov)
    chi_imag = (numer_imag + tikhonov * contrast[1]) / (weight + tikhonov)
    chi_power = chi_real * chi_real + chi_imag * chi_imag

    def norm_step(running, position):
        inc_real, inc_imag = incident(position)
        return (running + jnp.sum(chi_power * (inc_real * inc_real + inc_imag * inc_imag)), None)
    object_norm, unused = lax.scan(norm_step, jnp.zeros((), jnp.float32), positions)
    data_norm = jnp.sum(measured * measured)
    norm_ratio = object_norm / (data_norm + norm_floor)

    def update_step(running, step_items):
        source, scatter_pair, position, target, cell_index = step_items
        inc_real, inc_imag = incident(position)
        total_real = inc_real + scatter_pair[0]
        total_imag = inc_imag + scatter_pair[1]
        res_real = chi_real * total_real - chi_imag * total_imag - source[0]
        res_imag = chi_real * total_imag + chi_imag * total_real - source[1]
        flat_field = scatter_pair.reshape(2, NC * NC * NC)
        misfit = target - jnp.take(flat_field, cell_index, axis=1)
        placed = jnp.zeros((2, NC * NC * NC), jnp.float32).at[:, cell_index].add(misfit).reshape(2, NC, NC, NC)
        drive_real = norm_ratio * placed[0] - (chi_real * res_real + chi_imag * res_imag)
        drive_imag = norm_ratio * placed[1] - (chi_real * res_imag - chi_imag * res_real)
        back_real, back_imag = convolve(drive_real, drive_imag, spectrum[0], -spectrum[1])
        updated = jnp.stack([source[0] + step_length * (res_real + back_real), source[1] + step_length * (res_imag + back_imag)])
        return (running, updated)
    unused, sources_new = lax.scan(update_step, jnp.zeros((), jnp.float32), (sources, scattered, positions, measured, receivers))
    return (sources_new, jnp.stack([chi_real, chi_imag]))
```

```python
import functools
import math

import jax
import jax.numpy as jnp
import numpy as np
from jax import lax
from jax.experimental import pallas as pl
from jax.experimental.pallas import tpu as pltpu
from jax.sharding import PartitionSpec as P

wave_number = 2.0 * math.pi / 12.0
reach_cells = 16.0
tikhonov = 1.0
step_length = 0.5
norm_floor = 1e-06

ROWS = 8
LANES = 128
UNROLL = 4
VMEM_LIMIT = 56 * 1024 * 1024
F32 = jnp.float32
BF16 = jnp.bfloat16


def two_parts(table):
    table = np.asarray(table, np.float64)
    high = table.astype(np.float32).astype(jnp.bfloat16)
    low = (table - high.astype(np.float64)).astype(np.float32).astype(jnp.bfloat16)
    return np.asarray(high), np.asarray(low)


def phases(rows, columns, period, sign, divisor):
    angle = (np.outer(rows, columns) % period) * (2.0 * np.pi / period)
    return np.cos(angle) / divisor, sign * np.sin(angle) / divisor


def left_table(rows, columns, period, sign, divisor):
    cos, sin = phases(rows, columns, period, sign, divisor)
    return np.concatenate([np.concatenate([cos, -sin], 1), np.concatenate([sin, cos], 1)], 0)


def right_table(rows, columns, period, sign, divisor):
    return left_table(columns, rows, period, sign, divisor).T


def spread_order(devices, cuts):
    order = np.arange(2 * devices * sum(cuts)).reshape(2, devices, sum(cuts))
    ends = np.cumsum(cuts)
    pieces = [order[:, :, end - cut : end] for cut, end in zip(cuts, ends)]
    return np.concatenate([piece.transpose(1, 0, 2).reshape(-1) for piece in pieces])


def split_order(devices, planes, pieces):
    order = np.arange(devices * planes).reshape(devices, pieces, planes // pieces)
    return order.transpose(1, 0, 2).reshape(-1)


def split(value):
    high = value.astype(BF16)
    return high, (value - high.astype(F32)).astype(BF16)


def mm(left, right):
    return jnp.dot(left, right, preferred_element_type=F32)


def three(left_high, left_low, right_high, right_low):
    return mm(left_high, right_high) + (mm(left_high, right_low) + mm(left_low, right_high))


def table_left(high, low, value):
    return three(high, low, *split(value))


def table_right(value, high, low):
    return three(*split(value), high, low)


def whole(array):
    return pl.BlockSpec(array.shape, lambda *i: (0,) * array.ndim)


def params():
    return pltpu.CompilerParams(vmem_limit_bytes=VMEM_LIMIT)


def side_by_side(planes):
    return jnp.concatenate(planes, 1) if len(planes) > 1 else planes[0]


def forward_rows(field, high, low, out_refs):
    stacked = jnp.concatenate([side_by_side(field[0]), side_by_side(field[1])], 0)
    product = table_left(high, low, stacked)
    first = 0
    for out_ref in out_refs:
        devices, planes, _, part, width = out_ref.shape
        count = devices * 2 * part
        for i in range(planes):
            piece = product[first : first + count, i * width : (i + 1) * width]
            out_ref[:, i] = piece.reshape(devices, 2, part, width)
        first += count


def first_kernel(src_ref, high_ref, low_ref, *out_refs):
    planes = src_ref.shape[1]
    field = [[src_ref[part, i] for i in range(planes)] for part in range(2)]
    forward_rows(field, high_ref[...], low_ref[...], out_refs)


def first_call(src, table, devices, cuts):
    _, planes, depth, width = src.shape
    step = 2 if planes % 2 == 0 else 1
    high, low = table
    return pl.pallas_call(
        first_kernel,
        grid=(planes // step,),
        in_specs=[
            pl.BlockSpec((2, step, depth, width), lambda i: (0, i, 0, 0)),
            whole(high),
            whole(low),
        ],
        out_specs=[
            pl.BlockSpec((devices, step, 2, cut, width), lambda i: (0, i, 0, 0, 0)) for cut in cuts
        ],
        out_shape=[jax.ShapeDtypeStruct((devices, planes, 2, cut, width), F32) for cut in cuts],
        compiler_params=params(),
    )(src, high, low)


def spectral_kernel(*refs, pieces_in, pieces_out, pieces_wide, sign, extra, carried):
    refs = list(refs)
    ins = [refs.pop(0) for _ in range(pieces_in)]
    if extra:
        add_ref, ratio_ref = refs.pop(0), refs.pop(0)
    specs = [refs.pop(0) for _ in range(pieces_wide)]
    tch, tcl, tah, tal, tiah, tial, tich, ticl = (refs.pop(0) for _ in range(8))
    refs = refs[carried:]
    outs = [refs.pop(0) for _ in range(pieces_out)]
    mid_high, mid_low, end_high, end_low = refs
    _, padded, rows, lanes = specs[0].shape
    domain = tial.shape[0] // 2
    width = ins[0].shape[-1]
    flat_in = [r.reshape(-1, width) for r in ins]
    flat_out = [r.reshape(-1, width) for r in outs]
    flat_spec = [r.reshape(2 * padded * rows, lanes) for r in specs]
    count_in, count_out = domain // pieces_in, domain // pieces_out

    def planes_in(j):
        parts = []
        for part in range(2):
            got = [r[pl.ds(part * rows + j, count_in, stride=2 * rows), :] for r in flat_in]
            parts.append(jnp.concatenate(got, 0) if len(got) > 1 else got[0])
        plane = jnp.concatenate(parts, 1)
        return plane + ratio_ref[0, 0] * add_ref[j] if extra else plane

    along_c = table_right(jnp.concatenate([planes_in(j) for j in range(rows)], 0), tch[...], tcl[...])
    for j in range(rows):
        piece = along_c[j * domain : (j + 1) * domain]
        high, low = split(piece)
        for part in range(2):
            lanes_of = slice(part * padded, (part + 1) * padded)
            mid_high[j, part * domain : (part + 1) * domain] = high[:, lanes_of]
            mid_low[j, part * domain : (part + 1) * domain] = low[:, lanes_of]

    def body(j, carry):
        full = three(tah[...], tal[...], mid_high[j], mid_low[j])
        real, imag = full[:padded], full[padded:]
        spec_real, spec_imag = (
            side_by_side([r[pl.ds(p * padded * rows + j, padded, stride=rows), :] for r in flat_spec])
            for p in range(2)
        )
        if sign > 0:
            new_real = real * spec_real - imag * spec_imag
            new_imag = real * spec_imag + imag * spec_real
        else:
            new_real = real * spec_real + imag * spec_imag
            new_imag = imag * spec_real - real * spec_imag
        back = table_left(tiah[...], tial[...], jnp.concatenate([new_real, new_imag], 0))
        high, low = split(jnp.concatenate([back[:domain], back[domain:]], 1))
        start = pl.multiple_of(j * domain, domain)
        end_high[pl.ds(start, domain), :] = high
        end_low[pl.ds(start, domain), :] = low
        return carry

    lax.fori_loop(0, rows, body, 0, unroll=UNROLL)
    result = three(end_high[...], end_low[...], tich[...], ticl[...])
    for j in range(rows):
        for part in range(2):
            for h, r in enumerate(flat_out):
                first = j * domain + h * count_out
                r[pl.ds(part * rows + j, count_out, stride=2 * rows), :] = result[
                    first : first + count_out, part * width : (part + 1) * width
                ]


def spectral_call(
    pieces, spectrum, tables, pieces_out, planes, sign, rows_in, rows_of, total, add=None, ratio=None, before=()
):
    devices, planes_in, _, _, width = pieces[0].shape
    _, padded, _, _ = spectrum.shape
    planes_out = planes // pieces_out
    first, count = rows_of
    rows = ROWS if count % ROWS == 0 else count
    domain = devices * planes
    out_first, out_total = total

    def exchange(planes_here, start):
        return pl.BlockSpec(
            (devices, planes_here, 2, rows, width), lambda i: (0, 0, 0, start // rows + i, 0)
        )

    operands = list(pieces)
    in_specs = [exchange(planes_in, rows_in)] * len(pieces)
    if add is not None:
        operands += [add, ratio]
        in_specs += [
            pl.BlockSpec((rows, domain, 2 * width), lambda i: (first // rows + i, 0, 0)),
            pl.BlockSpec(memory_space=pltpu.SMEM),
        ]
    lanes = LANES if padded % LANES == 0 else padded
    for k in range(padded // lanes):
        operands.append(spectrum)
        in_specs.append(
            pl.BlockSpec((2, padded, rows, lanes), lambda i, k=k: (0, 0, first // rows + i, k))
        )
    for table in tables:
        for piece in table:
            operands.append(piece)
            in_specs.append(whole(piece))
    aliases = {len(operands) + k: k for k in range(len(before))}
    operands += before
    in_specs += [pl.BlockSpec(memory_space=pl.ANY)] * len(before)
    kernel = functools.partial(
        spectral_kernel,
        pieces_in=len(pieces),
        pieces_out=pieces_out,
        pieces_wide=padded // lanes,
        sign=sign,
        extra=add is not None,
        carried=len(before),
    )
    flops = count * 1536 * 6 * padded * padded
    shape = (devices, planes_out, 2, out_total, width)
    return pl.pallas_call(
        kernel,
        grid=(count // rows,),
        in_specs=in_specs,
        out_specs=[exchange(planes_out, out_first)] * pieces_out,
        out_shape=[jax.ShapeDtypeStruct(shape, F32)] * pieces_out,
        input_output_aliases=aliases,
        scratch_shapes=[pltpu.VMEM((rows, 2 * domain, padded), BF16)] * 2
        + [pltpu.VMEM((rows * domain, 2 * padded), BF16)] * 2,
        compiler_params=params(),
        cost_estimate=pl.CostEstimate(
            flops=flops, bytes_accessed=count * padded * padded * 16, transcendentals=0
        ),
    )(*operands)


def inverse_rows(got_refs, high, low):
    _, planes, _, _, width = got_refs[0].shape
    stacked = jnp.concatenate(
        [side_by_side([r[:, i].reshape(-1, width) for i in range(planes)]) for r in got_refs], 0
    )
    product = table_left(high, low, stacked)
    depth = product.shape[0] // 2
    return [
        [product[p * depth : (p + 1) * depth, i * width : (i + 1) * width] for i in range(planes)]
        for p in range(2)
    ]


def total_kernel(got_ref, src_ref, inc_ref, high_ref, low_ref, *refs):
    scat_ref, sums_ref = refs[-2:]
    scat = inverse_rows([got_ref], high_ref[...], low_ref[...])
    for i in range(src_ref.shape[1]):
        scat_real, scat_imag = scat[0][i], scat[1][i]
        scat_ref[0, i], scat_ref[1, i] = scat_real, scat_imag
        total_real, total_imag = inc_ref[0, i] + scat_real, inc_ref[1, i] + scat_imag
        src_real, src_imag = src_ref[0, i], src_ref[1, i]
        sums_ref[0, i] = src_real * total_real + src_imag * total_imag
        sums_ref[1, i] = src_imag * total_real - src_real * total_imag
        sums_ref[2, i] = total_real * total_real + total_imag * total_imag


def plane_spec(lead, step, depth, width, first):
    return pl.BlockSpec((lead, step, depth, width), lambda i: (0, first + i, 0, 0))


def step_of(planes):
    return 2 if planes % 2 == 0 else 1


def total_call(got, src, inc, table, piece, scat=None):
    devices, planes, _, part, width = got.shape
    _, all_planes, depth, _ = src.shape
    step = step_of(planes)
    first = piece * planes // step
    high, low = table
    there = plane_spec(2, step, depth, width, first)
    operands = [got, src, inc, high, low]
    in_specs = [
        pl.BlockSpec((devices, step, 2, part, width), lambda i: (0, i, 0, 0, 0)),
        there,
        there,
        whole(high),
        whole(low),
    ]
    aliases = {}
    if scat is not None:
        operands.append(scat)
        in_specs.append(pl.BlockSpec(memory_space=pl.ANY))
        aliases = {5: 0}
    return pl.pallas_call(
        total_kernel,
        grid=(planes // step,),
        in_specs=in_specs,
        out_specs=[there, plane_spec(3, step, depth, width, 0)],
        out_shape=[
            jax.ShapeDtypeStruct(src.shape, F32),
            jax.ShapeDtypeStruct((3, planes, depth, width), F32),
        ],
        input_output_aliases=aliases,
        compiler_params=params(),
    )(*operands)


def drive_kernel(sums_ref, con_ref, src_ref, inc_ref, power_ref, scat_ref, high_ref, low_ref, *refs):
    out_ref, chi_ref, base_ref, norm_ref = refs[-4:]
    planes = src_ref.shape[1]
    drive = [[], []]
    norm = jnp.zeros(norm_ref.shape, F32)
    for i in range(planes):
        weight = sums_ref[2, i] + tikhonov
        chi_real = (sums_ref[0, i] + tikhonov * con_ref[0, i]) / weight
        chi_imag = (sums_ref[1, i] + tikhonov * con_ref[1, i]) / weight
        chi_ref[0, i], chi_ref[1, i] = chi_real, chi_imag
        spread = (chi_real * chi_real + chi_imag * chi_imag) * power_ref[0, i]
        norm = norm + jnp.sum(spread.reshape((-1,) + norm.shape), 0)
        total_real = inc_ref[0, i] + scat_ref[0, i]
        total_imag = inc_ref[1, i] + scat_ref[1, i]
        src_real, src_imag = src_ref[0, i], src_ref[1, i]
        res_real = chi_real * total_real - chi_imag * total_imag - src_real
        res_imag = chi_real * total_imag + chi_imag * total_real - src_imag
        base_ref[0, i] = src_real + step_length * res_real
        base_ref[1, i] = src_imag + step_length * res_imag
        drive[0].append(-(chi_real * res_real + chi_imag * res_imag))
        drive[1].append(chi_imag * res_real - chi_real * res_imag)
    forward_rows(drive, high_ref[...], low_ref[...], [out_ref])

    @pl.when(pl.program_id(0) == 0)
    def start():
        norm_ref[...] = norm

    @pl.when(pl.program_id(0) > 0)
    def add():
        norm_ref[...] += norm


def drive_call(sums, contrast, src, inc, power, scat, table, devices, part, piece, before=()):
    _, planes, depth, width = sums.shape
    step = step_of(planes)
    first = piece * planes // step
    high, low = table
    there = plane_spec(2, step, depth, width, first)
    operands = [sums, contrast, src, inc, power, scat, high, low, *before]
    in_specs = [
        plane_spec(3, step, depth, width, 0),
        there,
        there,
        there,
        plane_spec(1, step, depth, width, first),
        there,
        whole(high),
        whole(low),
    ] + [pl.BlockSpec(memory_space=pl.ANY)] * len(before)
    return pl.pallas_call(
        drive_kernel,
        grid=(planes // step,),
        in_specs=in_specs,
        out_specs=[
            pl.BlockSpec((devices, step, 2, part, width), lambda i: (0, i, 0, 0, 0)),
            there,
            there,
            pl.BlockSpec((8, width), lambda i: (0, 0)),
        ],
        out_shape=[
            jax.ShapeDtypeStruct((devices, planes, 2, part, width), F32),
            jax.ShapeDtypeStruct(src.shape, F32),
            jax.ShapeDtypeStruct(src.shape, F32),
            jax.ShapeDtypeStruct((8, width), F32),
        ],
        input_output_aliases={8: 1, 9: 2} if before else {},
        compiler_params=params(),
    )(*operands)


def last_kernel(*refs):
    *got_refs, base_ref, high_ref, low_ref, out_ref = refs
    back = inverse_rows(got_refs, high_ref[...], low_ref[...])
    for part in range(2):
        for i in range(base_ref.shape[1]):
            out_ref[part, i] = base_ref[part, i] + step_length * back[part][i]


def last_call(gots, base, table):
    _, planes, depth, width = base.shape
    step = step_of(planes)
    high, low = table
    there = plane_spec(2, step, depth, width, 0)
    return pl.pallas_call(
        last_kernel,
        grid=(planes // step,),
        in_specs=[
            pl.BlockSpec((got.shape[0], step, 2, got.shape[3], width), lambda i: (0, i, 0, 0, 0))
            for got in gots
        ]
        + [there, whole(high), whole(low)],
        out_specs=there,
        out_shape=jax.ShapeDtypeStruct(base.shape, F32),
        compiler_params=params(),
    )(*gots, base, high, low)


def sample_kernel(index_ref, field_ref, out_ref):
    _, planes, depth, width = field_ref.shape
    count = out_ref.shape[0]
    rows = planes * depth
    field = jnp.concatenate([field_ref[p].reshape(rows, width) for p in range(2)], 1)
    at = lax.broadcasted_iota(jnp.int32, (count, rows), 1) + pl.program_id(0) * rows
    at = jnp.where(at == index_ref[...], 1.0, 0.0).astype(BF16)
    high, rest = split(field)
    low = field - high.astype(F32) - rest.astype(F32)
    got = mm(at, high) + (mm(at, rest) + mm(at, low.astype(BF16)))

    @pl.when(pl.program_id(0) == 0)
    def start():
        out_ref[...] = got

    @pl.when(pl.program_id(0) > 0)
    def add():
        out_ref[...] += got


def sample_call(index, field, first, planes):
    _, _, depth, width = field.shape
    count = index.shape[0]
    step = step_of(planes)
    return pl.pallas_call(
        sample_kernel,
        grid=(planes // step,),
        in_specs=[whole(index), plane_spec(2, step, depth, width, first // step)],
        out_specs=pl.BlockSpec((count, 2 * width), lambda i: (0, 0)),
        out_shape=jax.ShapeDtypeStruct((count, 2 * width), F32),
        compiler_params=params(),
    )(index, field)


def placed_kernel(row_ref, column_ref, turned_ref, out_ref):
    rows, domain, _ = out_ref.shape
    count = row_ref.shape[1]
    width = out_ref.shape[2] // 2
    at_a = lax.broadcasted_iota(jnp.int32, (domain, count), 0) == row_ref[...]
    at_a = jnp.where(at_a, 1.0, 0.0).astype(BF16)
    at_c = lax.broadcasted_iota(jnp.int32, (width, count), 0) == column_ref[...]
    at_c = jnp.where(at_c, 1.0, 0.0)
    contract = (((1,), (1,)), ((), ()))
    for j in range(rows):
        field = jnp.concatenate([at_c * turned_ref[0, pl.ds(j, 1)], at_c * turned_ref[1, pl.ds(j, 1)]], 0)
        high, low = split(field)
        out_ref[j] = lax.dot_general(
            at_a, high, contract, preferred_element_type=F32
        ) + lax.dot_general(at_a, low, contract, preferred_element_type=F32)


def placed_call(row, column, turned, domain, width):
    _, part, count = turned.shape
    rows = ROWS if part % ROWS == 0 else part
    return pl.pallas_call(
        placed_kernel,
        grid=(part // rows,),
        in_specs=[
            whole(row),
            whole(column),
            pl.BlockSpec((2, rows, count), lambda i: (0, i, 0)),
        ],
        out_specs=pl.BlockSpec((rows, domain, 2 * width), lambda i: (i, 0, 0)),
        out_shape=jax.ShapeDtypeStruct((part, domain, 2 * width), F32),
        compiler_params=params(),
    )(row, column, turned)


def shards(devices, sources, contrast, spectrum, measured, receivers, positions):
    src = sources.reshape(sources.shape[1:])
    _, planes, depth, width = src.shape
    _, padded, part, _ = spectrum.shape
    domain = devices * planes
    halves = 2 if planes % 2 == 0 else 1
    place = lax.axis_index("gz")
    offset = place * planes

    natural = np.arange(domain)
    cut = split_order(devices, planes, halves)
    wide = np.arange(padded)
    if part % ROWS == 0 and part > ROWS:
        cuts_out, cuts_back = (part - ROWS, ROWS), (ROWS, part - ROWS)
    else:
        cuts_out = cuts_back = (part,)

    def forward_b(cuts):
        table = left_table(wide, np.arange(depth), padded, -1.0, 1.0)
        return two_parts(table[spread_order(devices, cuts)])

    def inverse_b(cuts):
        table = left_table(np.arange(depth), wide, padded, 1.0, padded)
        return two_parts(table[:, spread_order(devices, cuts)])

    forward_c = two_parts(right_table(np.arange(width), wide, padded, -1.0, 1.0))
    inverse_c = two_parts(right_table(wide, np.arange(width), padded, 1.0, padded))

    def along_a(order_in, order_out):
        return (
            forward_c,
            two_parts(left_table(wide, order_in, padded, -1.0, 1.0)),
            two_parts(left_table(order_out, wide, padded, 1.0, padded)),
            inverse_c,
        )

    def exchange(array):
        return lax.all_to_all(array, "gz", 0, 0)

    def after(value, *others):
        return lax.optimization_barrier((value, *others))[0]

    sent = first_call(src, forward_b(cuts_out), devices, cuts_out)
    gots = [exchange(piece) for piece in sent]

    shape = (planes, depth, width)
    first_axis = lax.broadcasted_iota(jnp.int32, shape, 0) + offset + depth // 4

    def radius_of(position):
        second = lax.broadcasted_iota(jnp.int32, shape, 1) - position[0]
        third = lax.broadcasted_iota(jnp.int32, shape, 2) - position[1]
        squared = first_axis * first_axis + second * second + third * third
        return jnp.sqrt(squared.astype(F32))

    radius = radius_of(positions[0])
    amplitude = reach_cells / (reach_cells + radius)
    angle = wave_number * radius
    inc = jnp.stack([amplitude * jnp.cos(angle), amplitude * jnp.sin(angle)])
    everywhere = lax.all_gather(positions, "tx", axis=0, tiled=True)
    power = jnp.zeros(shape, F32)
    for j in range(everywhere.shape[0]):
        level = reach_cells / (reach_cells + radius_of(everywhere[j]))
        power = power + level * level
    power = power[None]
    data_norm = lax.psum(jnp.sum(measured * measured), "tx")

    cell = receivers[0]
    row, rest = cell // (depth * width), cell % (depth * width)
    second, third = rest // width, rest % width
    rows_kb = place * part + lax.broadcasted_iota(jnp.int32, (part, cell.shape[0]), 0)
    turn = (rows_kb * second[None] % padded).astype(F32) * (2.0 * math.pi / padded)
    cos, sin = jnp.cos(turn), jnp.sin(turn)
    device_of, plane_of = row // planes, row % planes
    piece_planes = planes // halves
    row_place = (plane_of // piece_planes) * (devices * piece_planes) + device_of * piece_planes
    row_place = row_place + plane_of % piece_planes
    lane = lax.broadcasted_iota(jnp.int32, (cell.shape[0], width), 1) == third[:, None]

    gots[0], inc, power, data_norm, cos, sin = lax.optimization_barrier(
        (gots[0], inc, power, data_norm, cos, sin)
    )

    tables, outs, first = along_a(natural, cut), (), 0
    for got, count in zip(gots, cuts_out):
        outs = spectral_call(
            [got], spectrum, tables, halves, planes, 1.0, 0, (first, count), (first, part), before=outs
        )
        first += count
    gots = [exchange(piece) for piece in outs]

    inverse_all, forward_all = inverse_b((part,)), forward_b((part,))
    scat, summed, carried, sends, norms = None, None, (), [], []
    seen = jnp.zeros((cell.shape[0], 2 * width), F32)
    for h in range(halves):
        scat, sums = total_call(gots[h], src, inc, inverse_all, h, scat)
        if summed is not None:
            sums = after(sums, summed)
        summed = lax.psum(sums, "tx")
        begin = h * piece_planes
        inside = (row - offset >= begin) & (row - offset < begin + piece_planes)
        index = jnp.where(inside, (row - offset - begin) * depth + second, -1)
        seen = seen + sample_call(index[:, None], scat, begin, piece_planes)
        if h == halves - 1:
            picked = [jnp.sum(jnp.where(lane, seen[:, p * width : (p + 1) * width], 0.0), 1) for p in range(2)]
            sampled = lax.psum(jnp.stack(picked), "gz")
            summed, sampled = lax.optimization_barrier((summed, sampled))
        send, chi, base, norm = drive_call(
            summed, contrast, src, inc, power, scat, forward_all, devices, part, h, carried
        )
        carried = (chi, base)
        sends.append(exchange(send))
        norms.append(norm)
    chi, base = carried

    misfit = measured[0] - sampled
    turned = jnp.stack(
        [misfit[:1] * cos + misfit[1:] * sin, misfit[1:] * cos - misfit[:1] * sin]
    )
    add = placed_call(row_place[None], third[None], turned, domain, width)
    object_norm = lax.psum(jnp.sum(sum(norms)), "gz")
    ratio = object_norm / (data_norm + norm_floor)
    ratio = ratio.reshape(1, 1)

    tables, gots, first = along_a(cut, natural), [], 0
    for count in cuts_back:
        (out,) = spectral_call(
            sends, spectrum, tables, 1, planes, -1.0, first, (first, count), (0, count), add, ratio
        )
        gots.append(exchange(out))
        first += count
    new = last_call(gots, base, inverse_b(cuts_back))
    return new[None], chi


def solution(mesh):
    in_specs = (
        P("tx", None, "gz", None, None),
        P(None, "gz", None, None),
        P(None, None, "gz", None),
        P("tx", None, None),
        P("tx", None),
        P("tx", None),
    )
    out_specs = (P("tx", None, "gz", None, None), P(None, "gz", None, None))
    body = functools.partial(shards, mesh.shape["gz"])
    return jax.shard_map(body, mesh=mesh, in_specs=in_specs, out_specs=out_specs, check_vma=False)
```

```python
import functools
import math

import jax
import jax.numpy as jnp
import numpy as np
from jax import lax
from jax.experimental import pallas as pl
from jax.experimental.pallas import tpu as pltpu
from jax.sharding import PartitionSpec as P

wave_number = 2.0 * math.pi / 12.0
reach_cells = 16.0
tikhonov = 1.0
step_length = 0.5
norm_floor = 1e-06

ROWS = 8
LANES = 128
UNROLL = 4
VMEM_LIMIT = 63 * 1024 * 1024
F32 = jnp.float32
BF16 = jnp.bfloat16


def two_parts(table):
    table = np.asarray(table, np.float64)
    high = table.astype(np.float32).astype(jnp.bfloat16)
    low = (table - high.astype(np.float64)).astype(np.float32).astype(jnp.bfloat16)
    return np.asarray(high), np.asarray(low)


def phases(rows, columns, period, sign, divisor):
    angle = (np.outer(rows, columns) % period) * (2.0 * np.pi / period)
    return np.cos(angle) / divisor, sign * np.sin(angle) / divisor


def left_table(rows, columns, period, sign, divisor):
    cos, sin = phases(rows, columns, period, sign, divisor)
    return np.concatenate([np.concatenate([cos, -sin], 1), np.concatenate([sin, cos], 1)], 0)


def right_table(rows, columns, period, sign, divisor):
    return left_table(columns, rows, period, sign, divisor).T


def spread_order(devices, cuts):
    order = np.arange(2 * devices * sum(cuts)).reshape(2, devices, sum(cuts))
    ends = np.cumsum(cuts)
    pieces = [order[:, :, end - cut : end] for cut, end in zip(cuts, ends)]
    return np.concatenate([piece.transpose(1, 0, 2).reshape(-1) for piece in pieces])


def split_order(devices, planes, pieces):
    order = np.arange(devices * planes).reshape(devices, pieces, planes // pieces)
    return order.transpose(1, 0, 2).reshape(-1)


def split(value):
    high = value.astype(BF16)
    return high, (value - high.astype(F32)).astype(BF16)


def mm(left, right):
    return jnp.dot(left, right, preferred_element_type=F32)


def three(left_high, left_low, right_high, right_low):
    return mm(left_high, right_high) + (mm(left_high, right_low) + mm(left_low, right_high))


def table_left(high, low, value):
    return three(high, low, *split(value))


def table_right(value, high, low):
    return three(*split(value), high, low)


def whole(array):
    return pl.BlockSpec(array.shape, lambda *i: (0,) * array.ndim)


def params():
    return pltpu.CompilerParams(vmem_limit_bytes=VMEM_LIMIT)


def cost(factor, *arrays):
    size = sum(4 * math.prod(array.shape) for array in arrays)
    return pl.CostEstimate(flops=0, bytes_accessed=int(factor * size), transcendentals=0)


def side_by_side(planes):
    return jnp.concatenate(planes, 1) if len(planes) > 1 else planes[0]


def forward_rows(field, high, low, out_refs):
    stacked = jnp.concatenate([side_by_side(field[0]), side_by_side(field[1])], 0)
    product = table_left(high, low, stacked)
    first = 0
    for out_ref in out_refs:
        devices, planes, _, part, width = out_ref.shape
        count = devices * 2 * part
        for i in range(planes):
            piece = product[first : first + count, i * width : (i + 1) * width]
            out_ref[:, i] = piece.reshape(devices, 2, part, width)
        first += count


def first_kernel(src_ref, high_ref, low_ref, *out_refs):
    planes = src_ref.shape[1]
    field = [[src_ref[part, i] for i in range(planes)] for part in range(2)]
    forward_rows(field, high_ref[...], low_ref[...], out_refs)


def first_call(src, table, devices, cuts):
    _, planes, depth, width = src.shape
    step = 2 if planes % 2 == 0 else 1
    high, low = table
    return pl.pallas_call(
        first_kernel,
        grid=(planes // step,),
        in_specs=[
            pl.BlockSpec((2, step, depth, width), lambda i: (0, i, 0, 0)),
            whole(high),
            whole(low),
        ],
        out_specs=[
            pl.BlockSpec((devices, step, 2, cut, width), lambda i: (0, i, 0, 0, 0)) for cut in cuts
        ],
        out_shape=[jax.ShapeDtypeStruct((devices, planes, 2, cut, width), F32) for cut in cuts],
        compiler_params=params(),
        cost_estimate=cost(12, src),
    )(src, high, low)


def spectral_kernel(*refs, pieces_in, pieces_out, pieces_wide, sign, extra, carried):
    refs = list(refs)
    ins = [refs.pop(0) for _ in range(pieces_in)]
    if extra:
        add_ref, ratio_ref = refs.pop(0), refs.pop(0)
    specs = [refs.pop(0) for _ in range(pieces_wide)]
    tch, tcl, tah, tal, tiah, tial, tich, ticl = (refs.pop(0) for _ in range(8))
    refs = refs[carried:]
    outs = [refs.pop(0) for _ in range(pieces_out)]
    mid_high, mid_low, end_high, end_low = refs
    _, padded, rows, lanes = specs[0].shape
    domain = tial.shape[0] // 2
    width = ins[0].shape[-1]
    flat_in = [r.reshape(-1, width) for r in ins]
    flat_out = [r.reshape(-1, width) for r in outs]
    flat_spec = [r.reshape(2 * padded * rows, lanes) for r in specs]
    count_in, count_out = domain // pieces_in, domain // pieces_out

    def planes_in(j):
        parts = []
        for part in range(2):
            got = [r[pl.ds(part * rows + j, count_in, stride=2 * rows), :] for r in flat_in]
            parts.append(jnp.concatenate(got, 0) if len(got) > 1 else got[0])
        plane = jnp.concatenate(parts, 1)
        return plane + ratio_ref[0, 0] * add_ref[j] if extra else plane

    along_c = table_right(jnp.concatenate([planes_in(j) for j in range(rows)], 0), tch[...], tcl[...])
    for j in range(rows):
        piece = along_c[j * domain : (j + 1) * domain]
        high, low = split(piece)
        for part in range(2):
            lanes_of = slice(part * padded, (part + 1) * padded)
            mid_high[j, part * domain : (part + 1) * domain] = high[:, lanes_of]
            mid_low[j, part * domain : (part + 1) * domain] = low[:, lanes_of]

    def body(j, carry):
        chunk = padded // 2
        back = None
        for c in range(2):
            picked = [slice(p * padded + c * chunk, p * padded + (c + 1) * chunk) for p in range(2)]
            high = jnp.concatenate([tah[r, :] for r in picked], 0)
            low = jnp.concatenate([tal[r, :] for r in picked], 0)
            full = three(high, low, mid_high[j], mid_low[j])
            real, imag = full[:chunk], full[chunk:]
            spec_real, spec_imag = (
                side_by_side([r[pl.ds(p.start * rows + j, chunk, stride=rows), :] for r in flat_spec])
                for p in picked
            )
            if sign > 0:
                new_real = real * spec_real - imag * spec_imag
                new_imag = real * spec_imag + imag * spec_real
            else:
                new_real = real * spec_real + imag * spec_imag
                new_imag = imag * spec_real - real * spec_imag
            high = jnp.concatenate([tiah[:, r] for r in picked], 1)
            low = jnp.concatenate([tial[:, r] for r in picked], 1)
            term = table_left(high, low, jnp.concatenate([new_real, new_imag], 0))
            back = term if back is None else back + term
        high, low = split(jnp.concatenate([back[:domain], back[domain:]], 1))
        start = pl.multiple_of(j * domain, domain)
        end_high[pl.ds(start, domain), :] = high
        end_low[pl.ds(start, domain), :] = low
        return carry

    lax.fori_loop(0, rows, body, 0, unroll=UNROLL)
    result = three(end_high[...], end_low[...], tich[...], ticl[...])
    for j in range(rows):
        for part in range(2):
            for h, r in enumerate(flat_out):
                first = j * domain + h * count_out
                r[pl.ds(part * rows + j, count_out, stride=2 * rows), :] = result[
                    first : first + count_out, part * width : (part + 1) * width
                ]


def spectral_call(
    pieces, spectrum, tables, pieces_out, planes, sign, rows_in, rows_of, total, add=None, ratio=None, before=()
):
    devices, planes_in, _, _, width = pieces[0].shape
    _, padded, part, _ = spectrum.shape
    planes_out = planes // pieces_out
    first, count = rows_of
    rows = ROWS if count % ROWS == 0 else count
    domain = devices * planes
    out_first, out_total = total

    def exchange(planes_here, start):
        return pl.BlockSpec(
            (devices, planes_here, 2, rows, width), lambda i: (0, 0, 0, start // rows + i, 0)
        )

    operands = list(pieces)
    in_specs = [exchange(planes_in, rows_in)] * len(pieces)
    if add is not None:
        operands += [add, ratio]
        in_specs += [
            pl.BlockSpec((rows, domain, 2 * width), lambda i: (first // rows + i, 0, 0)),
            pl.BlockSpec(memory_space=pltpu.SMEM),
        ]
    lanes = LANES if padded % LANES == 0 else padded
    for k in range(padded // lanes):
        operands.append(spectrum)
        in_specs.append(
            pl.BlockSpec((2, padded, rows, lanes), lambda i, k=k: (0, 0, first // rows + i, k))
        )
    for table in tables:
        for piece in table:
            operands.append(piece)
            in_specs.append(whole(piece))
    aliases = {len(operands) + k: k for k in range(len(before))}
    operands += before
    in_specs += [pl.BlockSpec(memory_space=pl.ANY)] * len(before)
    kernel = functools.partial(
        spectral_kernel,
        pieces_in=len(pieces),
        pieces_out=pieces_out,
        pieces_wide=padded // lanes,
        sign=sign,
        extra=add is not None,
        carried=len(before),
    )
    shape = (devices, planes_out, 2, out_total, width)
    return pl.pallas_call(
        kernel,
        grid=(count // rows,),
        in_specs=in_specs,
        out_specs=[exchange(planes_out, out_first)] * pieces_out,
        out_shape=[jax.ShapeDtypeStruct(shape, F32)] * pieces_out,
        input_output_aliases=aliases,
        scratch_shapes=[pltpu.VMEM((rows, 2 * domain, padded), BF16)] * 2
        + [pltpu.VMEM((rows * domain, 2 * padded), BF16)] * 2,
        compiler_params=params(),
        cost_estimate=cost(8 * count / part, spectrum),
    )(*operands)


def inverse_rows(got_refs, high, low):
    _, planes, _, _, width = got_refs[0].shape
    stacked = jnp.concatenate(
        [side_by_side([r[:, i].reshape(-1, width) for i in range(planes)]) for r in got_refs], 0
    )
    product = table_left(high, low, stacked)
    depth = product.shape[0] // 2
    return [
        [product[p * depth : (p + 1) * depth, i * width : (i + 1) * width] for i in range(planes)]
        for p in range(2)
    ]


def total_kernel(got_ref, src_ref, inc_ref, high_ref, low_ref, *refs):
    scat_ref, sums_ref = refs[-2:]
    scat = inverse_rows([got_ref], high_ref[...], low_ref[...])
    for i in range(src_ref.shape[1]):
        scat_real, scat_imag = scat[0][i], scat[1][i]
        scat_ref[0, i], scat_ref[1, i] = scat_real, scat_imag
        total_real, total_imag = inc_ref[0, i] + scat_real, inc_ref[1, i] + scat_imag
        src_real, src_imag = src_ref[0, i], src_ref[1, i]
        sums_ref[0, i] = src_real * total_real + src_imag * total_imag
        sums_ref[1, i] = src_imag * total_real - src_real * total_imag
        sums_ref[2, i] = total_real * total_real + total_imag * total_imag


def plane_spec(lead, step, depth, width, first):
    return pl.BlockSpec((lead, step, depth, width), lambda i: (0, first + i, 0, 0))


def step_of(planes, most=2):
    return next(step for step in (most, 2, 1) if planes % step == 0)


def total_call(got, src, inc, table, piece, scat=None):
    devices, planes, _, part, width = got.shape
    _, all_planes, depth, _ = src.shape
    step = step_of(planes)
    first = piece * planes // step
    high, low = table
    there = plane_spec(2, step, depth, width, first)
    operands = [got, src, inc, high, low]
    in_specs = [
        pl.BlockSpec((devices, step, 2, part, width), lambda i: (0, i, 0, 0, 0)),
        there,
        there,
        whole(high),
        whole(low),
    ]
    aliases = {}
    if scat is not None:
        operands.append(scat)
        in_specs.append(pl.BlockSpec(memory_space=pl.ANY))
        aliases = {5: 0}
    return pl.pallas_call(
        total_kernel,
        grid=(planes // step,),
        in_specs=in_specs,
        out_specs=[there, plane_spec(3, step, depth, width, 0)],
        out_shape=[
            jax.ShapeDtypeStruct(src.shape, F32),
            jax.ShapeDtypeStruct((3, planes, depth, width), F32),
        ],
        input_output_aliases=aliases,
        compiler_params=params(),
        cost_estimate=cost(9, got),
    )(*operands)


def drive_kernel(own_ref, mine_ref, other_ref, con_ref, src_ref, inc_ref, power_ref, scat_ref, high_ref, low_ref, *refs):
    out_ref, chi_ref, base_ref, norm_ref = refs[-4:]
    planes = src_ref.shape[1]
    half = (pl.program_id(0) * 2) // pl.num_programs(0)
    is_mine = half == own_ref[0, 0]
    sums_ref = jnp.where(is_mine, mine_ref[...], other_ref[...])
    drive = [[], []]
    norm = jnp.zeros(norm_ref.shape, F32)
    for i in range(planes):
        weight = sums_ref[2, i] + tikhonov
        chi_real = (sums_ref[0, i] + tikhonov * con_ref[0, i]) / weight
        chi_imag = (sums_ref[1, i] + tikhonov * con_ref[1, i]) / weight
        chi_ref[0, i], chi_ref[1, i] = chi_real, chi_imag
        spread = (chi_real * chi_real + chi_imag * chi_imag) * power_ref[0, i]
        norm = norm + jnp.sum(spread.reshape((-1,) + norm.shape), 0)
        total_real = inc_ref[0, i] + scat_ref[0, i]
        total_imag = inc_ref[1, i] + scat_ref[1, i]
        src_real, src_imag = src_ref[0, i], src_ref[1, i]
        res_real = chi_real * total_real - chi_imag * total_imag - src_real
        res_imag = chi_real * total_imag + chi_imag * total_real - src_imag
        base_ref[0, i] = src_real + step_length * res_real
        base_ref[1, i] = src_imag + step_length * res_imag
        drive[0].append(-(chi_real * res_real + chi_imag * res_imag))
        drive[1].append(chi_imag * res_real - chi_real * res_imag)
    forward_rows(drive, high_ref[...], low_ref[...], [out_ref])

    @pl.when(pl.program_id(0) == 0)
    def start():
        norm_ref[...] = norm

    @pl.when(pl.program_id(0) > 0)
    def add():
        norm_ref[...] += norm


def drive_call(sums, contrast, src, inc, power, scat, table, devices, part, piece, before=()):
    mine, other, own = sums
    _, half_planes, depth, width = mine.shape
    planes = 2 * half_planes
    step = step_of(half_planes)
    first = piece * planes // step
    high, low = table
    there = plane_spec(2, step, depth, width, first)
    operands = [own, mine, other, contrast, src, inc, power, scat, high, low, *before]
    halved = pl.BlockSpec((3, step, depth, width), lambda i: (0, i % (half_planes // step), 0, 0))
    in_specs = [
        pl.BlockSpec(memory_space=pltpu.SMEM),
        halved,
        halved,
        there,
        there,
        there,
        plane_spec(1, step, depth, width, first),
        there,
        whole(high),
        whole(low),
    ] + [pl.BlockSpec(memory_space=pl.ANY)] * len(before)
    return pl.pallas_call(
        drive_kernel,
        grid=(planes // step,),
        in_specs=in_specs,
        out_specs=[
            pl.BlockSpec((devices, step, 2, part, width), lambda i: (0, i, 0, 0, 0)),
            there,
            there,
            pl.BlockSpec((8, width), lambda i: (0, 0)),
        ],
        out_shape=[
            jax.ShapeDtypeStruct((devices, planes, 2, part, width), F32),
            jax.ShapeDtypeStruct(src.shape, F32),
            jax.ShapeDtypeStruct(src.shape, F32),
            jax.ShapeDtypeStruct((8, width), F32),
        ],
        input_output_aliases={10: 1, 11: 2} if before else {},
        compiler_params=params(),
        cost_estimate=cost(16, mine),
    )(*operands)


def last_kernel(*refs):
    *got_refs, base_ref, high_ref, low_ref, out_ref = refs
    back = inverse_rows(got_refs, high_ref[...], low_ref[...])
    for part in range(2):
        for i in range(base_ref.shape[1]):
            out_ref[part, i] = base_ref[part, i] + step_length * back[part][i]


def last_call(gots, base, table):
    _, planes, depth, width = base.shape
    step = step_of(planes, 4)
    high, low = table
    there = plane_spec(2, step, depth, width, 0)
    return pl.pallas_call(
        last_kernel,
        grid=(planes // step,),
        in_specs=[
            pl.BlockSpec((got.shape[0], step, 2, got.shape[3], width), lambda i: (0, i, 0, 0, 0))
            for got in gots
        ]
        + [there, whole(high), whole(low)],
        out_specs=there,
        out_shape=jax.ShapeDtypeStruct(base.shape, F32),
        compiler_params=params(),
        cost_estimate=cost(12, base),
    )(*gots, base, high, low)


def sample_kernel(index_ref, field_ref, out_ref):
    _, planes, depth, width = field_ref.shape
    count = out_ref.shape[0]
    rows = planes * depth
    field = jnp.concatenate([field_ref[p].reshape(rows, width) for p in range(2)], 1)
    at = lax.broadcasted_iota(jnp.int32, (count, rows), 1) + pl.program_id(0) * rows
    at = jnp.where(at == index_ref[...], 1.0, 0.0).astype(BF16)
    high, rest = split(field)
    low = field - high.astype(F32) - rest.astype(F32)
    got = mm(at, high) + (mm(at, rest) + mm(at, low.astype(BF16)))

    @pl.when(pl.program_id(0) == 0)
    def start():
        out_ref[...] = got

    @pl.when(pl.program_id(0) > 0)
    def add():
        out_ref[...] += got


def sample_call(index, field):
    _, planes, depth, width = field.shape
    count = index.shape[0]
    step = step_of(planes)
    return pl.pallas_call(
        sample_kernel,
        grid=(planes // step,),
        in_specs=[whole(index), plane_spec(2, step, depth, width, 0)],
        out_specs=pl.BlockSpec((count, 2 * width), lambda i: (0, 0)),
        out_shape=jax.ShapeDtypeStruct((count, 2 * width), F32),
        compiler_params=params(),
        cost_estimate=cost(16, field),
    )(index, field)


def placed_kernel(row_ref, column_ref, turned_ref, out_ref):
    rows, domain, _ = out_ref.shape
    count = row_ref.shape[1]
    width = out_ref.shape[2] // 2
    at_a = lax.broadcasted_iota(jnp.int32, (domain, count), 0) == row_ref[...]
    at_a = jnp.where(at_a, 1.0, 0.0).astype(BF16)
    at_c = lax.broadcasted_iota(jnp.int32, (width, count), 0) == column_ref[...]
    at_c = jnp.where(at_c, 1.0, 0.0)
    contract = (((1,), (1,)), ((), ()))
    for j in range(rows):
        field = jnp.concatenate([at_c * turned_ref[0, pl.ds(j, 1)], at_c * turned_ref[1, pl.ds(j, 1)]], 0)
        high, low = split(field)
        out_ref[j] = lax.dot_general(
            at_a, high, contract, preferred_element_type=F32
        ) + lax.dot_general(at_a, low, contract, preferred_element_type=F32)


def placed_call(row, column, turned, domain, width):
    _, part, count = turned.shape
    rows = ROWS if part % ROWS == 0 else part
    return pl.pallas_call(
        placed_kernel,
        grid=(part // rows,),
        in_specs=[
            whole(row),
            whole(column),
            pl.BlockSpec((2, rows, count), lambda i: (0, i, 0)),
        ],
        out_specs=pl.BlockSpec((rows, domain, 2 * width), lambda i: (i, 0, 0)),
        out_shape=jax.ShapeDtypeStruct((part, domain, 2 * width), F32),
        compiler_params=params(),
        cost_estimate=pl.CostEstimate(
            flops=12 * part * domain * 2 * width * count, bytes_accessed=0, transcendentals=0
        ),
    )(row, column, turned)


def flipped(value, axis, count, bits):
    return lax.ppermute(value, axis, [(i, i ^ bits) for i in range(count)])


def sum_staged(value, axis, count, ends=(0, None)):
    if count & (count - 1):
        return lax.psum(value, axis) if ends[0] == 0 else value
    stages, low, width = [], 1, 2
    while low < count:
        width = min(width, count // low)
        stages.append([k * low for k in range(1, width)])
        low, width = low * width, 4
    for stage in stages[ends[0] : ends[1]]:
        value = value + sum(flipped(value, axis, count, bits) for bits in stage)
    return value


def sum_halved(value, axis, count, beside=()):
    half = value.shape[1] // 2
    if count & (count - 1) or count < 2 or value.shape[1] % 2:
        value = lax.psum(value, axis)
        return value[:, :half], value[:, half:], jnp.zeros((1, 1), jnp.int32)
    me = lax.axis_index(axis) % 2
    mine = lax.dynamic_slice_in_dim(value, me * half, half, 1)
    other = lax.dynamic_slice_in_dim(value, (1 - me) * half, half, 1)
    mine = mine + flipped(other, axis, count, 1)
    low = 2
    while low < count:
        got, *beside = lax.optimization_barrier((flipped(mine, axis, count, low), *beside))
        mine = mine + got
        low *= 2
    return mine, flipped(mine, axis, count, 1), me.astype(jnp.int32).reshape(1, 1)


def shards(transmitters, devices, sources, contrast, spectrum, measured, receivers, positions):
    src = sources.reshape(sources.shape[1:])
    _, planes, depth, width = src.shape
    _, padded, part, _ = spectrum.shape
    domain = devices * planes
    halves = 2 if planes % 2 == 0 else 1
    place = lax.axis_index("gz")
    offset = place * planes

    natural = np.arange(domain)
    cut = split_order(devices, planes, halves)
    wide = np.arange(padded)
    if part % ROWS == 0 and part > ROWS:
        cuts_out, cuts_back = (part - ROWS, ROWS), (ROWS, part - ROWS)
    else:
        cuts_out = cuts_back = (part,)

    def forward_b(cuts):
        table = left_table(wide, np.arange(depth), padded, -1.0, 1.0)
        return two_parts(table[spread_order(devices, cuts)])

    def inverse_b(cuts):
        table = left_table(np.arange(depth), wide, padded, 1.0, padded)
        return two_parts(table[:, spread_order(devices, cuts)])

    forward_c = two_parts(right_table(np.arange(width), wide, padded, -1.0, 1.0))
    inverse_c = two_parts(right_table(wide, np.arange(width), padded, 1.0, padded))

    def along_a(order_in, order_out):
        return (
            forward_c,
            two_parts(left_table(wide, order_in, padded, -1.0, 1.0)),
            two_parts(left_table(order_out, wide, padded, 1.0, padded)),
            inverse_c,
        )

    def exchange(array):
        return lax.all_to_all(array, "gz", 0, 0)

    sent = first_call(src, forward_b(cuts_out), devices, cuts_out)
    gots = [exchange(sent[0])]

    shape = (planes, depth, width)
    first_axis = lax.broadcasted_iota(jnp.int32, shape, 0) + offset + depth // 4

    def radius_of(position):
        second = lax.broadcasted_iota(jnp.int32, shape, 1) - position[0]
        third = lax.broadcasted_iota(jnp.int32, shape, 2) - position[1]
        squared = first_axis * first_axis + second * second + third * third
        return jnp.sqrt(squared.astype(F32))

    radius = radius_of(positions[0])
    amplitude = reach_cells / (reach_cells + radius)
    angle = wave_number * radius
    inc = jnp.stack([amplitude * jnp.cos(angle), amplitude * jnp.sin(angle)])
    everywhere = lax.all_gather(positions, "tx", axis=0, tiled=True)
    power = jnp.zeros(shape, F32)
    for j in range(everywhere.shape[0]):
        level = reach_cells / (reach_cells + radius_of(everywhere[j]))
        power = power + level * level
    power = power[None]
    data_norm = lax.psum(jnp.sum(measured * measured), "tx")

    cell = receivers[0]
    row, rest = cell // (depth * width), cell % (depth * width)
    second, third = rest // width, rest % width
    rows_kb = place * part + lax.broadcasted_iota(jnp.int32, (part, cell.shape[0]), 0)
    turn = (rows_kb * second[None] % padded).astype(F32) * (2.0 * math.pi / padded)
    cos, sin = jnp.cos(turn), jnp.sin(turn)
    device_of, plane_of = row // planes, row % planes
    piece_planes = planes // halves
    row_place = (plane_of // piece_planes) * (devices * piece_planes) + device_of * piece_planes
    row_place = row_place + plane_of % piece_planes
    lane = lax.broadcasted_iota(jnp.int32, (cell.shape[0], width), 1) == third[:, None]

    if len(cuts_out) > 1:
        last, inc, power, data_norm, cos, sin = lax.optimization_barrier(
            (sent[1], inc, power, data_norm, cos, sin)
        )
        gots.append(exchange(last))

    tables, outs, first = along_a(natural, cut), (), 0
    for got, count in zip(gots, cuts_out):
        outs = spectral_call(
            [got], spectrum, tables, halves, planes, 1.0, 0, (first, count), (first, part), before=outs
        )
        first += count
    gots = [exchange(piece) for piece in outs]

    inverse_all, forward_all = inverse_b((part,)), forward_b((part,))
    scat, summed, carried, sends, norms = None, None, (), [], []
    for h in range(halves):
        scat, sums = total_call(gots[h], src, inc, inverse_all, h, scat)
        if h < halves - 1:
            summed = sum_halved(sums, "tx", transmitters)
        else:
            inside = (row >= offset) & (row < offset + planes)
            index = jnp.where(inside, (row - offset) * depth + second, -1)
            got = sample_call(index[:, None], scat)
            seen = [jnp.sum(jnp.where(lane, got[:, p * width : (p + 1) * width], 0.0), 1) for p in range(2)]
            seen = jnp.stack(seen)
            seen = sum_staged(seen, "gz", devices, (0, 1))
            summed = sum_halved(sums, "tx", transmitters, [seen])
            seen = sum_staged(seen, "gz", devices, (1, None))
        send, chi, base, norm = drive_call(
            summed, contrast, src, inc, power, scat, forward_all, devices, part, h, carried
        )
        carried = (chi, base)
        if h == halves - 1:
            send, seen = lax.optimization_barrier((send, seen))
        sends.append(exchange(send))
        norms.append(norm)
    chi, base = carried

    misfit = measured[0] - seen
    turned = jnp.stack(
        [misfit[:1] * cos + misfit[1:] * sin, misfit[1:] * cos - misfit[:1] * sin]
    )
    add = placed_call(row_place[None], third[None], turned, domain, width)
    object_norm = sum_staged(jnp.sum(sum(norms)).reshape(1, 1), "gz", devices)
    ratio = object_norm / (data_norm + norm_floor)

    tables, gots, first = along_a(cut, natural), [], 0
    for count in cuts_back:
        (out,) = spectral_call(
            sends, spectrum, tables, 1, planes, -1.0, first, (first, count), (0, count), add, ratio
        )
        gots.append(exchange(out))
        first += count
    new = last_call(gots, base, inverse_b(cuts_back))
    return new[None], chi


def solution(mesh):
    in_specs = (
        P("tx", None, "gz", None, None),
        P(None, "gz", None, None),
        P(None, None, "gz", None),
        P("tx", None, None),
        P("tx", None),
        P("tx", None),
    )
    out_specs = (P("tx", None, "gz", None, None), P(None, "gz", None, None))
    body = functools.partial(shards, mesh.shape["tx"], mesh.shape["gz"])
    return jax.shard_map(body, mesh=mesh, in_specs=in_specs, out_specs=out_specs, check_vma=False)
```

```python
import functools
import math

import jax
import jax.numpy as jnp
import numpy as np
from jax import lax
from jax.experimental import pallas as pl
from jax.experimental.pallas import tpu as pltpu
from jax.sharding import PartitionSpec as P

wave_number = 2.0 * math.pi / 12.0
reach_cells = 16.0
tikhonov = 1.0
step_length = 0.5
norm_floor = 1e-06

ROWS = 8
LANES = 128
UNROLL = 4
VMEM_LIMIT = 63 * 1024 * 1024
F32 = jnp.float32
BF16 = jnp.bfloat16


def two_parts(table):
    table = np.asarray(table, np.float64)
    high = table.astype(np.float32).astype(jnp.bfloat16)
    low = (table - high.astype(np.float64)).astype(np.float32).astype(jnp.bfloat16)
    return np.asarray(high), np.asarray(low)


def phases(rows, columns, period, sign, divisor):
    angle = (np.outer(rows, columns) % period) * (2.0 * np.pi / period)
    return np.cos(angle) / divisor, sign * np.sin(angle) / divisor


def left_table(rows, columns, period, sign, divisor):
    cos, sin = phases(rows, columns, period, sign, divisor)
    return np.concatenate([np.concatenate([cos, -sin], 1), np.concatenate([sin, cos], 1)], 0)


def right_table(rows, columns, period, sign, divisor):
    return left_table(columns, rows, period, sign, divisor).T


def spread_order(devices, cuts):
    order = np.arange(2 * devices * sum(cuts)).reshape(2, devices, sum(cuts))
    ends = np.cumsum(cuts)
    pieces = [order[:, :, end - cut : end] for cut, end in zip(cuts, ends)]
    return np.concatenate([piece.transpose(1, 0, 2).reshape(-1) for piece in pieces])


def split_order(devices, planes, pieces):
    order = np.arange(devices * planes).reshape(devices, pieces, planes // pieces)
    return order.transpose(1, 0, 2).reshape(-1)


def split(value):
    high = value.astype(BF16)
    return high, (value - high.astype(F32)).astype(BF16)


def mm(left, right):
    return jnp.dot(left, right, preferred_element_type=F32)


def three(left_high, left_low, right_high, right_low):
    return mm(left_high, right_high) + (mm(left_high, right_low) + mm(left_low, right_high))


def table_left(high, low, value):
    return three(high, low, *split(value))


def table_right(value, high, low):
    return three(*split(value), high, low)


def whole(array):
    return pl.BlockSpec(array.shape, lambda *i: (0,) * array.ndim)


def params():
    return pltpu.CompilerParams(vmem_limit_bytes=VMEM_LIMIT)


def cost(factor, *arrays):
    size = sum(4 * math.prod(array.shape) for array in arrays)
    return pl.CostEstimate(flops=0, bytes_accessed=int(factor * size), transcendentals=0)


def side_by_side(planes):
    return jnp.concatenate(planes, 1) if len(planes) > 1 else planes[0]


def forward_rows(field, high, low, out_refs):
    stacked = jnp.concatenate([side_by_side(field[0]), side_by_side(field[1])], 0)
    product = table_left(high, low, stacked)
    first = 0
    for out_ref in out_refs:
        devices, planes, _, part, width = out_ref.shape
        count = devices * 2 * part
        for i in range(planes):
            piece = product[first : first + count, i * width : (i + 1) * width]
            out_ref[:, i] = piece.reshape(devices, 2, part, width)
        first += count


def first_kernel(src_ref, high_ref, low_ref, *out_refs):
    planes = src_ref.shape[1]
    field = [[src_ref[part, i] for i in range(planes)] for part in range(2)]
    forward_rows(field, high_ref[...], low_ref[...], out_refs)


def first_call(src, table, devices, cuts):
    _, planes, depth, width = src.shape
    step = 2 if planes % 2 == 0 else 1
    high, low = table
    return pl.pallas_call(
        first_kernel,
        grid=(planes // step,),
        in_specs=[
            pl.BlockSpec((2, step, depth, width), lambda i: (0, i, 0, 0)),
            whole(high),
            whole(low),
        ],
        out_specs=[
            pl.BlockSpec((devices, step, 2, cut, width), lambda i: (0, i, 0, 0, 0)) for cut in cuts
        ],
        out_shape=[jax.ShapeDtypeStruct((devices, planes, 2, cut, width), F32) for cut in cuts],
        compiler_params=params(),
        cost_estimate=cost(12, src),
    )(src, high, low)


def spectral_kernel(*refs, pieces_in, pieces_out, pieces_wide, sign, extra, carried):
    refs = list(refs)
    ins = [refs.pop(0) for _ in range(pieces_in)]
    if extra:
        add_ref, ratio_ref = refs.pop(0), refs.pop(0)
    specs = [refs.pop(0) for _ in range(pieces_wide)]
    tch, tcl, tah, tal, tiah, tial, tich, ticl = (refs.pop(0) for _ in range(8))
    refs = refs[carried:]
    outs = [refs.pop(0) for _ in range(pieces_out)]
    mid_high, mid_low, end_high, end_low = refs
    _, padded, rows, lanes = specs[0].shape
    domain = tial.shape[0] // 2
    width = ins[0].shape[-1]
    flat_in = [r.reshape(-1, width) for r in ins]
    flat_out = [r.reshape(-1, width) for r in outs]
    flat_spec = [r.reshape(2 * padded * rows, lanes) for r in specs]
    count_in, count_out = domain // pieces_in, domain // pieces_out

    def planes_in(j):
        parts = []
        for part in range(2):
            got = [r[pl.ds(part * rows + j, count_in, stride=2 * rows), :] for r in flat_in]
            parts.append(jnp.concatenate(got, 0) if len(got) > 1 else got[0])
        plane = jnp.concatenate(parts, 1)
        return plane + ratio_ref[0, 0] * add_ref[j] if extra else plane

    along_c = table_right(jnp.concatenate([planes_in(j) for j in range(rows)], 0), tch[...], tcl[...])
    for j in range(rows):
        piece = along_c[j * domain : (j + 1) * domain]
        high, low = split(piece)
        for part in range(2):
            lanes_of = slice(part * padded, (part + 1) * padded)
            mid_high[j, part * domain : (part + 1) * domain] = high[:, lanes_of]
            mid_low[j, part * domain : (part + 1) * domain] = low[:, lanes_of]

    def body(j, carry):
        chunk = padded // 2
        back = None
        for c in range(2):
            picked = [slice(p * padded + c * chunk, p * padded + (c + 1) * chunk) for p in range(2)]
            high = jnp.concatenate([tah[r, :] for r in picked], 0)
            low = jnp.concatenate([tal[r, :] for r in picked], 0)
            full = three(high, low, mid_high[j], mid_low[j])
            real, imag = full[:chunk], full[chunk:]
            spec_real, spec_imag = (
                side_by_side([r[pl.ds(p.start * rows + j, chunk, stride=rows), :] for r in flat_spec])
                for p in picked
            )
            if sign > 0:
                new_real = real * spec_real - imag * spec_imag
                new_imag = real * spec_imag + imag * spec_real
            else:
                new_real = real * spec_real + imag * spec_imag
                new_imag = imag * spec_real - real * spec_imag
            high = jnp.concatenate([tiah[:, r] for r in picked], 1)
            low = jnp.concatenate([tial[:, r] for r in picked], 1)
            term = table_left(high, low, jnp.concatenate([new_real, new_imag], 0))
            back = term if back is None else back + term
        high, low = split(jnp.concatenate([back[:domain], back[domain:]], 1))
        start = pl.multiple_of(j * domain, domain)
        end_high[pl.ds(start, domain), :] = high
        end_low[pl.ds(start, domain), :] = low
        return carry

    lax.fori_loop(0, rows, body, 0, unroll=UNROLL)
    result = three(end_high[...], end_low[...], tich[...], ticl[...])
    for j in range(rows):
        for part in range(2):
            for h, r in enumerate(flat_out):
                first = j * domain + h * count_out
                r[pl.ds(part * rows + j, count_out, stride=2 * rows), :] = result[
                    first : first + count_out, part * width : (part + 1) * width
                ]


def spectral_call(
    pieces, spectrum, tables, planes, sign, rows_in, rows_of, totals, add=None, ratio=None, before=()
):
    devices, planes_in, _, _, width = pieces[0].shape
    _, padded, part, _ = spectrum.shape
    pieces_out = len(totals)
    planes_out = planes // pieces_out
    first, count = rows_of
    rows = ROWS if count % ROWS == 0 else count
    domain = devices * planes

    def exchange(planes_here, start):
        return pl.BlockSpec(
            (devices, planes_here, 2, rows, width), lambda i: (0, 0, 0, start // rows + i, 0)
        )

    operands = list(pieces)
    in_specs = [exchange(planes_in, rows_in)] * len(pieces)
    if add is not None:
        operands += [add, ratio]
        in_specs += [
            pl.BlockSpec((rows, domain, 2 * width), lambda i: (first // rows + i, 0, 0)),
            pl.BlockSpec(memory_space=pltpu.SMEM),
        ]
    lanes = LANES if padded % LANES == 0 else padded
    for k in range(padded // lanes):
        operands.append(spectrum)
        in_specs.append(
            pl.BlockSpec((2, padded, rows, lanes), lambda i, k=k: (0, 0, first // rows + i, k))
        )
    for table in tables:
        for piece in table:
            operands.append(piece)
            in_specs.append(whole(piece))
    kept = [k for k, array in enumerate(before) if array is not None]
    aliases = {len(operands) + n: k for n, k in enumerate(kept)}
    operands += [before[k] for k in kept]
    in_specs += [pl.BlockSpec(memory_space=pl.ANY)] * len(kept)
    kernel = functools.partial(
        spectral_kernel,
        pieces_in=len(pieces),
        pieces_out=pieces_out,
        pieces_wide=padded // lanes,
        sign=sign,
        extra=add is not None,
        carried=len(kept),
    )
    lead = (devices, planes_out, 2)
    return pl.pallas_call(
        kernel,
        grid=(count // rows,),
        in_specs=in_specs,
        out_specs=[exchange(planes_out, start) for start, _ in totals],
        out_shape=[jax.ShapeDtypeStruct((*lead, rows, width), F32) for _, rows in totals],
        input_output_aliases=aliases,
        scratch_shapes=[pltpu.VMEM((rows, 2 * domain, padded), BF16)] * 2
        + [pltpu.VMEM((rows * domain, 2 * padded), BF16)] * 2,
        compiler_params=params(),
        cost_estimate=cost(8 * count / part, spectrum),
    )(*operands)


def inverse_rows(got_refs, high, low):
    _, planes, _, _, width = got_refs[0].shape
    stacked = jnp.concatenate(
        [side_by_side([r[:, i].reshape(-1, width) for i in range(planes)]) for r in got_refs], 0
    )
    product = table_left(high, low, stacked)
    depth = product.shape[0] // 2
    return [
        [product[p * depth : (p + 1) * depth, i * width : (i + 1) * width] for i in range(planes)]
        for p in range(2)
    ]


def total_kernel(count, *refs):
    src_ref, inc_ref, high_ref, low_ref, *_ = refs[count:]
    scat_ref, sums_ref = refs[-2:]
    scat = inverse_rows(refs[:count], high_ref[...], low_ref[...])
    for i in range(src_ref.shape[1]):
        scat_real, scat_imag = scat[0][i], scat[1][i]
        scat_ref[0, i], scat_ref[1, i] = scat_real, scat_imag
        total_real, total_imag = inc_ref[0, i] + scat_real, inc_ref[1, i] + scat_imag
        src_real, src_imag = src_ref[0, i], src_ref[1, i]
        sums_ref[0, i] = src_real * total_real + src_imag * total_imag
        sums_ref[1, i] = src_imag * total_real - src_real * total_imag
        sums_ref[2, i] = total_real * total_real + total_imag * total_imag


def plane_spec(lead, step, depth, width, first):
    return pl.BlockSpec((lead, step, depth, width), lambda i: (0, first + i, 0, 0))


def step_of(planes, most=2):
    return next(step for step in (most, 2, 1) if planes % step == 0)


def total_call(gots, src, inc, table, piece, scat=None):
    devices, planes, _, _, width = gots[0].shape
    _, all_planes, depth, _ = src.shape
    step = step_of(planes)
    first = piece * planes // step
    high, low = table
    there = plane_spec(2, step, depth, width, first)
    operands = [*gots, src, inc, high, low]
    in_specs = [
        pl.BlockSpec((devices, step, 2, got.shape[3], width), lambda i: (0, i, 0, 0, 0)) for got in gots
    ] + [
        there,
        there,
        whole(high),
        whole(low),
    ]
    aliases = {}
    if scat is not None:
        aliases = {len(operands): 0}
        operands.append(scat)
        in_specs.append(pl.BlockSpec(memory_space=pl.ANY))
    return pl.pallas_call(
        functools.partial(total_kernel, len(gots)),
        grid=(planes // step,),
        in_specs=in_specs,
        out_specs=[there, plane_spec(3, step, depth, width, 0)],
        out_shape=[
            jax.ShapeDtypeStruct(src.shape, F32),
            jax.ShapeDtypeStruct((3, planes, depth, width), F32),
        ],
        input_output_aliases=aliases,
        compiler_params=params(),
        cost_estimate=cost(9, *gots),
    )(*operands)


def sums_here(own_ref, mine_ref, other_ref):
    half = (pl.program_id(0) * 2) // pl.num_programs(0)
    return jnp.where(half == own_ref[0, 0], mine_ref[...], other_ref[...])


def contrast_of(sums, con_ref, i):
    weight = sums[2, i] + tikhonov
    return tuple((sums[p, i] + tikhonov * con_ref[p, i]) / weight for p in range(2))


def norm_kernel(own_ref, mine_ref, other_ref, con_ref, power_ref, norm_ref):
    sums = sums_here(own_ref, mine_ref, other_ref)
    norm = jnp.zeros(norm_ref.shape, F32)
    for i in range(con_ref.shape[1]):
        chi_real, chi_imag = contrast_of(sums, con_ref, i)
        spread = (chi_real * chi_real + chi_imag * chi_imag) * power_ref[0, i]
        norm = norm + jnp.sum(spread.reshape((-1,) + norm.shape), 0)

    @pl.when(pl.program_id(0) == 0)
    def start():
        norm_ref[...] = norm

    @pl.when(pl.program_id(0) > 0)
    def add():
        norm_ref[...] += norm


def norm_call(sums, contrast, power, piece):
    mine, other, own = sums
    _, half_planes, depth, width = mine.shape
    step = step_of(half_planes, 4)
    first = piece * 2 * half_planes // step
    halved = pl.BlockSpec((3, step, depth, width), lambda i: (0, i % (half_planes // step), 0, 0))
    return pl.pallas_call(
        norm_kernel,
        grid=(2 * half_planes // step,),
        in_specs=[
            pl.BlockSpec(memory_space=pltpu.SMEM),
            halved,
            halved,
            plane_spec(2, step, depth, width, first),
            plane_spec(1, step, depth, width, first),
        ],
        out_specs=pl.BlockSpec((8, width), lambda i: (0, 0)),
        out_shape=jax.ShapeDtypeStruct((8, width), F32),
        compiler_params=params(),
        cost_estimate=cost(4, mine),
    )(own, mine, other, contrast, power)


def drive_kernel(own_ref, mine_ref, other_ref, con_ref, src_ref, inc_ref, scat_ref, high_ref, low_ref, *refs):
    out_ref, chi_ref, base_ref = refs[-3:]
    planes = src_ref.shape[1]
    sums_ref = sums_here(own_ref, mine_ref, other_ref)
    drive = [[], []]
    for i in range(planes):
        chi_real, chi_imag = contrast_of(sums_ref, con_ref, i)
        chi_ref[0, i], chi_ref[1, i] = chi_real, chi_imag
        total_real = inc_ref[0, i] + scat_ref[0, i]
        total_imag = inc_ref[1, i] + scat_ref[1, i]
        src_real, src_imag = src_ref[0, i], src_ref[1, i]
        res_real = chi_real * total_real - chi_imag * total_imag - src_real
        res_imag = chi_real * total_imag + chi_imag * total_real - src_imag
        base_ref[0, i] = src_real + step_length * res_real
        base_ref[1, i] = src_imag + step_length * res_imag
        drive[0].append(-(chi_real * res_real + chi_imag * res_imag))
        drive[1].append(chi_imag * res_real - chi_real * res_imag)
    forward_rows(drive, high_ref[...], low_ref[...], [out_ref])


def drive_call(sums, contrast, src, inc, scat, table, devices, part, piece, before=()):
    mine, other, own = sums
    _, half_planes, depth, width = mine.shape
    planes = 2 * half_planes
    step = step_of(half_planes)
    first = piece * planes // step
    high, low = table
    there = plane_spec(2, step, depth, width, first)
    operands = [own, mine, other, contrast, src, inc, scat, high, low, *before]
    halved = pl.BlockSpec((3, step, depth, width), lambda i: (0, i % (half_planes // step), 0, 0))
    in_specs = [
        pl.BlockSpec(memory_space=pltpu.SMEM),
        halved,
        halved,
        there,
        there,
        there,
        there,
        whole(high),
        whole(low),
    ] + [pl.BlockSpec(memory_space=pl.ANY)] * len(before)
    return pl.pallas_call(
        drive_kernel,
        grid=(planes // step,),
        in_specs=in_specs,
        out_specs=[
            pl.BlockSpec((devices, step, 2, part, width), lambda i: (0, i, 0, 0, 0)),
            there,
            there,
        ],
        out_shape=[
            jax.ShapeDtypeStruct((devices, planes, 2, part, width), F32),
            jax.ShapeDtypeStruct(src.shape, F32),
            jax.ShapeDtypeStruct(src.shape, F32),
        ],
        input_output_aliases={9: 1, 10: 2} if before else {},
        compiler_params=params(),
        cost_estimate=cost(16, mine),
    )(*operands)


def last_kernel(*refs):
    *got_refs, base_ref, high_ref, low_ref, out_ref = refs
    back = inverse_rows(got_refs, high_ref[...], low_ref[...])
    for part in range(2):
        for i in range(base_ref.shape[1]):
            out_ref[part, i] = base_ref[part, i] + step_length * back[part][i]


def last_call(gots, base, table):
    _, planes, depth, width = base.shape
    step = step_of(planes, 8)
    high, low = table
    there = plane_spec(2, step, depth, width, 0)
    return pl.pallas_call(
        last_kernel,
        grid=(planes // step,),
        in_specs=[
            pl.BlockSpec((got.shape[0], step, 2, got.shape[3], width), lambda i: (0, i, 0, 0, 0))
            for got in gots
        ]
        + [there, whole(high), whole(low)],
        out_specs=there,
        out_shape=jax.ShapeDtypeStruct(base.shape, F32),
        compiler_params=params(),
        cost_estimate=cost(12, base),
    )(*gots, base, high, low)


def sample_kernel(index_ref, field_ref, out_ref):
    _, planes, depth, width = field_ref.shape
    count = out_ref.shape[0]
    rows = planes * depth
    field = jnp.concatenate([field_ref[p].reshape(rows, width) for p in range(2)], 1)
    at = lax.broadcasted_iota(jnp.int32, (count, rows), 1) + pl.program_id(0) * rows
    at = jnp.where(at == index_ref[...], 1.0, 0.0).astype(BF16)
    high, rest = split(field)
    low = field - high.astype(F32) - rest.astype(F32)
    got = mm(at, high) + (mm(at, rest) + mm(at, low.astype(BF16)))

    @pl.when(pl.program_id(0) == 0)
    def start():
        out_ref[...] = got

    @pl.when(pl.program_id(0) > 0)
    def add():
        out_ref[...] += got


def sample_call(index, field):
    _, planes, depth, width = field.shape
    count = index.shape[0]
    step = step_of(planes)
    return pl.pallas_call(
        sample_kernel,
        grid=(planes // step,),
        in_specs=[whole(index), plane_spec(2, step, depth, width, 0)],
        out_specs=pl.BlockSpec((count, 2 * width), lambda i: (0, 0)),
        out_shape=jax.ShapeDtypeStruct((count, 2 * width), F32),
        compiler_params=params(),
        cost_estimate=cost(16, field),
    )(index, field)


def placed_kernel(row_ref, column_ref, turned_ref, out_ref):
    rows, domain, _ = out_ref.shape
    count = row_ref.shape[1]
    width = out_ref.shape[2] // 2
    at_a = lax.broadcasted_iota(jnp.int32, (domain, count), 0) == row_ref[...]
    at_a = jnp.where(at_a, 1.0, 0.0).astype(BF16)
    at_c = lax.broadcasted_iota(jnp.int32, (width, count), 0) == column_ref[...]
    at_c = jnp.where(at_c, 1.0, 0.0)
    contract = (((1,), (1,)), ((), ()))
    for j in range(rows):
        field = jnp.concatenate([at_c * turned_ref[0, pl.ds(j, 1)], at_c * turned_ref[1, pl.ds(j, 1)]], 0)
        high, low = split(field)
        out_ref[j] = lax.dot_general(
            at_a, high, contract, preferred_element_type=F32
        ) + lax.dot_general(at_a, low, contract, preferred_element_type=F32)


def placed_call(row, column, turned, domain, width):
    _, part, count = turned.shape
    rows = ROWS if part % ROWS == 0 else part
    return pl.pallas_call(
        placed_kernel,
        grid=(part // rows,),
        in_specs=[
            whole(row),
            whole(column),
            pl.BlockSpec((2, rows, count), lambda i: (0, i, 0)),
        ],
        out_specs=pl.BlockSpec((rows, domain, 2 * width), lambda i: (i, 0, 0)),
        out_shape=jax.ShapeDtypeStruct((part, domain, 2 * width), F32),
        compiler_params=params(),
        cost_estimate=pl.CostEstimate(
            flops=12 * part * domain * 2 * width * count, bytes_accessed=0, transcendentals=0
        ),
    )(row, column, turned)


def flipped(value, axis, count, bits):
    return lax.ppermute(value, axis, [(i, i ^ bits) for i in range(count)])


def stages_of(count):
    stages, low, width = [], 1, 2
    while low < count:
        width = min(width, count // low)
        stages.append([k * low for k in range(1, width)])
        low, width = low * width, 4
    return stages


def sum_begun(value, axis, count):
    if count & (count - 1):
        return lax.psum(value, axis), []
    *stages, last = stages_of(count)
    for stage in stages:
        value = value + sum(flipped(value, axis, count, bits) for bits in stage)
    return value, [flipped(value, axis, count, bits) for bits in last]


def sum_halved(value, axis, count, beside=()):
    half = value.shape[1] // 2
    if count & (count - 1) or count < 2 or value.shape[1] % 2:
        value = lax.psum(value, axis)
        return (value[:, :half], value[:, half:], jnp.zeros((1, 1), jnp.int32)), beside
    me = lax.axis_index(axis) % 2
    mine = lax.dynamic_slice_in_dim(value, me * half, half, 1)
    other = lax.dynamic_slice_in_dim(value, (1 - me) * half, half, 1)
    mine = mine + flipped(other, axis, count, 1)
    low = 2
    while low < count:
        got, *beside = lax.optimization_barrier((flipped(mine, axis, count, low), *beside))
        mine = mine + got
        low *= 2
    return (mine, flipped(mine, axis, count, 1), me.astype(jnp.int32).reshape(1, 1)), beside


def shards(transmitters, devices, sources, contrast, spectrum, measured, receivers, positions):
    src = sources.reshape(sources.shape[1:])
    _, planes, depth, width = src.shape
    _, padded, part, _ = spectrum.shape
    domain = devices * planes
    halves = 2 if planes % 2 == 0 else 1
    place = lax.axis_index("gz")
    offset = place * planes

    natural = np.arange(domain)
    cut = split_order(devices, planes, halves)
    wide = np.arange(padded)
    if part % ROWS == 0 and part > ROWS:
        cuts_out, cuts_back = (part - ROWS, ROWS), (ROWS, part - ROWS)
    else:
        cuts_out = cuts_back = (part,)

    def forward_b(cuts):
        table = left_table(wide, np.arange(depth), padded, -1.0, 1.0)
        return two_parts(table[spread_order(devices, cuts)])

    def inverse_b(cuts):
        table = left_table(np.arange(depth), wide, padded, 1.0, padded)
        return two_parts(table[:, spread_order(devices, cuts)])

    forward_c = two_parts(right_table(np.arange(width), wide, padded, -1.0, 1.0))
    inverse_c = two_parts(right_table(wide, np.arange(width), padded, 1.0, padded))

    def along_a(order_in, order_out):
        return (
            forward_c,
            two_parts(left_table(wide, order_in, padded, -1.0, 1.0)),
            two_parts(left_table(order_out, wide, padded, 1.0, padded)),
            inverse_c,
        )

    def exchange(array):
        return lax.all_to_all(array, "gz", 0, 0)

    sent = first_call(src, forward_b(cuts_out), devices, cuts_out)
    gots_out = [exchange(sent[0])]

    shape = (planes, depth, width)
    first_axis = lax.broadcasted_iota(jnp.int32, shape, 0) + offset + depth // 4

    def radius_of(position):
        second = lax.broadcasted_iota(jnp.int32, shape, 1) - position[0]
        third = lax.broadcasted_iota(jnp.int32, shape, 2) - position[1]
        squared = first_axis * first_axis + second * second + third * third
        return jnp.sqrt(squared.astype(F32))

    radius = radius_of(positions[0])
    amplitude = reach_cells / (reach_cells + radius)
    angle = wave_number * radius
    inc = jnp.stack([amplitude * jnp.cos(angle), amplitude * jnp.sin(angle)])
    everywhere = lax.all_gather(positions, "tx", axis=0, tiled=True)
    power = jnp.zeros(shape, F32)
    for j in range(everywhere.shape[0]):
        level = reach_cells / (reach_cells + radius_of(everywhere[j]))
        power = power + level * level
    power = power[None]
    data_norm = lax.psum(jnp.sum(measured * measured), "tx")

    cell = receivers[0]
    row, rest = cell // (depth * width), cell % (depth * width)
    second, third = rest // width, rest % width
    rows_kb = place * part + lax.broadcasted_iota(jnp.int32, (part, cell.shape[0]), 0)
    turn = (rows_kb * second[None] % padded).astype(F32) * (2.0 * math.pi / padded)
    cos, sin = jnp.cos(turn), jnp.sin(turn)
    device_of, plane_of = row // planes, row % planes
    piece_planes = planes // halves
    row_place = (plane_of // piece_planes) * (devices * piece_planes) + device_of * piece_planes
    row_place = row_place + plane_of % piece_planes
    lane = lax.broadcasted_iota(jnp.int32, (cell.shape[0], width), 1) == third[:, None]

    if len(cuts_out) > 1:
        last, inc, power, data_norm, cos, sin = lax.optimization_barrier(
            (sent[1], inc, power, data_norm, cos, sin)
        )
        gots_out.append(exchange(last))

    tables, outs, first = along_a(natural, cut), (None,) * halves, 0
    gots = [[] for _ in range(halves)]
    for got, count in zip(gots_out, cuts_out):
        totals = [(0, count)] + [(first, part)] * (halves - 1)
        outs = spectral_call(
            [got], spectrum, tables, planes, 1.0, 0, (first, count), totals, before=(None, *outs[1:])
        )
        sent_now = outs[0]
        if gots[0]:
            sent_now, gots[0][-1] = lax.optimization_barrier((sent_now, gots[0][-1]))
        gots[0].append(exchange(sent_now))
        first += count
    for h in range(1, halves):
        gots[h].append(exchange(outs[h]))

    forward_all = forward_b((part,))
    inverse_all = [inverse_b(cuts_out)] + [inverse_b((part,))] * (halves - 1)
    scat, summed, carried, sends, norms = None, None, (), [], []
    for h in range(halves):
        scat, sums = total_call(gots[h], src, inc, inverse_all[h], h, scat)
        if h < halves - 1:
            summed, _ = sum_halved(sums, "tx", transmitters)
        else:
            inside = (row >= offset) & (row < offset + planes)
            index = jnp.where(inside, (row - offset) * depth + second, -1)
            got = sample_call(index[:, None], scat)
            seen = [jnp.sum(jnp.where(lane, got[:, p * width : (p + 1) * width], 0.0), 1) for p in range(2)]
            seen = jnp.stack(seen)
            summed, (seen, *norms) = sum_halved(sums, "tx", transmitters, [seen, *norms])
        norms.append(norm_call(summed, contrast, power, h))
        if h == halves - 1:
            small = jnp.concatenate([seen.reshape(-1), sum(norms).reshape(-1)])
            small, arriving = sum_begun(small, "gz", devices)
        send, chi, base = drive_call(
            summed, contrast, src, inc, scat, forward_all, devices, part, h, carried
        )
        carried = (chi, base)
        if h == halves - 1:
            send, *arriving = lax.optimization_barrier((send, *arriving))
        sends.append(exchange(send))
    chi, base = carried

    small = small + sum(arriving)
    seen, norm = small[: seen.size].reshape(seen.shape), small[seen.size :]
    misfit = measured[0] - seen
    turned = jnp.stack(
        [misfit[:1] * cos + misfit[1:] * sin, misfit[1:] * cos - misfit[:1] * sin]
    )
    add = placed_call(row_place[None], third[None], turned, domain, width)
    ratio = jnp.sum(norm).reshape(1, 1) / (data_norm + norm_floor)

    tables, gots, first = along_a(cut, natural), [], 0
    for count in cuts_back:
        (out,) = spectral_call(
            sends, spectrum, tables, planes, -1.0, first, (first, count), [(0, count)], add, ratio
        )
        gots.append(exchange(out))
        first += count
    new = last_call(gots, base, inverse_b(cuts_back))
    return new[None], chi


def solution(mesh):
    in_specs = (
        P("tx", None, "gz", None, None),
        P(None, "gz", None, None),
        P(None, None, "gz", None),
        P("tx", None, None),
        P("tx", None),
        P("tx", None),
    )
    out_specs = (P("tx", None, "gz", None, None), P(None, "gz", None, None))
    body = functools.partial(shards, mesh.shape["tx"], mesh.shape["gz"])
    return jax.shard_map(body, mesh=mesh, in_specs=in_specs, out_specs=out_specs, check_vma=False)
```

```python
import functools
import math

import jax
import jax.numpy as jnp
import numpy as np
from jax import lax
from jax.experimental import pallas as pl
from jax.experimental.pallas import tpu as pltpu
from jax.sharding import PartitionSpec as P

wave_number = 2.0 * math.pi / 12.0
reach_cells = 16.0
tikhonov = 1.0
step_length = 0.5
norm_floor = 1e-06

ROWS = 8
LANES = 128
UNROLL = 4
VMEM_LIMIT = 63 * 1024 * 1024
F32 = jnp.float32
BF16 = jnp.bfloat16


def two_parts(table):
    table = np.asarray(table, np.float64)
    high = table.astype(np.float32).astype(jnp.bfloat16)
    low = (table - high.astype(np.float64)).astype(np.float32).astype(jnp.bfloat16)
    return np.asarray(high), np.asarray(low)


def phases(rows, columns, period, sign, divisor):
    angle = (np.outer(rows, columns) % period) * (2.0 * np.pi / period)
    return np.cos(angle) / divisor, sign * np.sin(angle) / divisor


def left_table(rows, columns, period, sign, divisor):
    cos, sin = phases(rows, columns, period, sign, divisor)
    return np.concatenate([np.concatenate([cos, -sin], 1), np.concatenate([sin, cos], 1)], 0)


def right_table(rows, columns, period, sign, divisor):
    return left_table(columns, rows, period, sign, divisor).T


def spread_order(devices, cuts):
    order = np.arange(2 * devices * sum(cuts)).reshape(2, devices, sum(cuts))
    ends = np.cumsum(cuts)
    pieces = [order[:, :, end - cut : end] for cut, end in zip(cuts, ends)]
    return np.concatenate([piece.transpose(1, 0, 2).reshape(-1) for piece in pieces])


def split_order(devices, planes, pieces):
    order = np.arange(devices * planes).reshape(devices, pieces, planes // pieces)
    return order.transpose(1, 0, 2).reshape(-1)


def split(value):
    high = value.astype(BF16)
    return high, (value - high.astype(F32)).astype(BF16)


def mm(left, right):
    return jnp.dot(left, right, preferred_element_type=F32)


def three(left_high, left_low, right_high, right_low):
    return mm(left_high, right_high) + (mm(left_high, right_low) + mm(left_low, right_high))


def table_left(high, low, value):
    return three(high, low, *split(value))


def table_right(value, high, low):
    return three(*split(value), high, low)


def whole(array):
    return pl.BlockSpec(array.shape, lambda *i: (0,) * array.ndim)


def params():
    return pltpu.CompilerParams(vmem_limit_bytes=VMEM_LIMIT)


def cost(factor, *arrays):
    size = sum(4 * math.prod(array.shape) for array in arrays)
    return pl.CostEstimate(flops=0, bytes_accessed=int(factor * size), transcendentals=0)


def side_by_side(planes):
    return jnp.concatenate(planes, 1) if len(planes) > 1 else planes[0]


def forward_rows(field, high, low, out_refs):
    stacked = jnp.concatenate([side_by_side(field[0]), side_by_side(field[1])], 0)
    product = table_left(high, low, stacked)
    first = 0
    for out_ref in out_refs:
        devices, planes, _, part, width = out_ref.shape
        count = devices * 2 * part
        for i in range(planes):
            piece = product[first : first + count, i * width : (i + 1) * width]
            out_ref[:, i] = piece.reshape(devices, 2, part, width)
        first += count


def first_kernel(src_ref, high_ref, low_ref, *out_refs):
    planes = src_ref.shape[1]
    field = [[src_ref[part, i] for i in range(planes)] for part in range(2)]
    forward_rows(field, high_ref[...], low_ref[...], out_refs)


def first_call(src, table, devices, cuts):
    _, planes, depth, width = src.shape
    step = 2 if planes % 2 == 0 else 1
    high, low = table
    return pl.pallas_call(
        first_kernel,
        grid=(planes // step,),
        in_specs=[
            pl.BlockSpec((2, step, depth, width), lambda i: (0, i, 0, 0)),
            whole(high),
            whole(low),
        ],
        out_specs=[
            pl.BlockSpec((devices, step, 2, cut, width), lambda i: (0, i, 0, 0, 0)) for cut in cuts
        ],
        out_shape=[jax.ShapeDtypeStruct((devices, planes, 2, cut, width), F32) for cut in cuts],
        compiler_params=params(),
        cost_estimate=cost(12, src),
    )(src, high, low)


def spectral_kernel(*refs, pieces_in, pieces_out, pieces_wide, sign, extra, carried):
    refs = list(refs)
    ins = [refs.pop(0) for _ in range(pieces_in)]
    if extra:
        add_ref, ratio_ref = refs.pop(0), refs.pop(0)
    specs = [refs.pop(0) for _ in range(pieces_wide)]
    tch, tcl, tah, tal, tiah, tial, tich, ticl = (refs.pop(0) for _ in range(8))
    refs = refs[carried:]
    outs = [refs.pop(0) for _ in range(pieces_out)]
    mid_high, mid_low, end_high, end_low = refs
    _, padded, rows, lanes = specs[0].shape
    domain = tial.shape[0] // 2
    width = ins[0].shape[-1]
    flat_in = [r.reshape(-1, width) for r in ins]
    flat_out = [r.reshape(-1, width) for r in outs]
    flat_spec = [r.reshape(2 * padded * rows, lanes) for r in specs]
    count_in, count_out = domain // pieces_in, domain // pieces_out

    def planes_in(j):
        parts = []
        for part in range(2):
            got = [r[pl.ds(part * rows + j, count_in, stride=2 * rows), :] for r in flat_in]
            parts.append(jnp.concatenate(got, 0) if len(got) > 1 else got[0])
        plane = jnp.concatenate(parts, 1)
        return plane + ratio_ref[0, 0] * add_ref[j] if extra else plane

    along_c = table_right(jnp.concatenate([planes_in(j) for j in range(rows)], 0), tch[...], tcl[...])
    for j in range(rows):
        piece = along_c[j * domain : (j + 1) * domain]
        high, low = split(piece)
        for part in range(2):
            lanes_of = slice(part * padded, (part + 1) * padded)
            mid_high[j, part * domain : (part + 1) * domain] = high[:, lanes_of]
            mid_low[j, part * domain : (part + 1) * domain] = low[:, lanes_of]

    def body(j, carry):
        chunk = padded // 2
        back = None
        for c in range(2):
            picked = [slice(p * padded + c * chunk, p * padded + (c + 1) * chunk) for p in range(2)]
            high = jnp.concatenate([tah[r, :] for r in picked], 0)
            low = jnp.concatenate([tal[r, :] for r in picked], 0)
            full = three(high, low, mid_high[j], mid_low[j])
            real, imag = full[:chunk], full[chunk:]
            spec_real, spec_imag = (
                side_by_side([r[pl.ds(p.start * rows + j, chunk, stride=rows), :] for r in flat_spec])
                for p in picked
            )
            if sign > 0:
                new_real = real * spec_real - imag * spec_imag
                new_imag = real * spec_imag + imag * spec_real
            else:
                new_real = real * spec_real + imag * spec_imag
                new_imag = imag * spec_real - real * spec_imag
            high = jnp.concatenate([tiah[:, r] for r in picked], 1)
            low = jnp.concatenate([tial[:, r] for r in picked], 1)
            term = table_left(high, low, jnp.concatenate([new_real, new_imag], 0))
            back = term if back is None else back + term
        high, low = split(jnp.concatenate([back[:domain], back[domain:]], 1))
        start = pl.multiple_of(j * domain, domain)
        end_high[pl.ds(start, domain), :] = high
        end_low[pl.ds(start, domain), :] = low
        return carry

    lax.fori_loop(0, rows, body, 0, unroll=UNROLL)
    result = three(end_high[...], end_low[...], tich[...], ticl[...])
    for j in range(rows):
        for part in range(2):
            for h, r in enumerate(flat_out):
                first = j * domain + h * count_out
                r[pl.ds(part * rows + j, count_out, stride=2 * rows), :] = result[
                    first : first + count_out, part * width : (part + 1) * width
                ]


def spectral_call(
    pieces, spectrum, tables, planes, sign, rows_in, rows_of, totals, add=None, ratio=None, before=()
):
    devices, planes_in, _, _, width = pieces[0].shape
    _, padded, part, _ = spectrum.shape
    pieces_out = len(totals)
    planes_out = planes // pieces_out
    first, count = rows_of
    rows = ROWS if count % ROWS == 0 else count
    domain = devices * planes

    def exchange(planes_here, start):
        return pl.BlockSpec(
            (devices, planes_here, 2, rows, width), lambda i: (0, 0, 0, start // rows + i, 0)
        )

    operands = list(pieces)
    in_specs = [exchange(planes_in, start) for start in rows_in]
    if add is not None:
        operands += [add, ratio]
        in_specs += [
            pl.BlockSpec((rows, domain, 2 * width), lambda i: (first // rows + i, 0, 0)),
            pl.BlockSpec(memory_space=pltpu.SMEM),
        ]
    lanes = LANES if padded % LANES == 0 else padded
    for k in range(padded // lanes):
        operands.append(spectrum)
        in_specs.append(
            pl.BlockSpec((2, padded, rows, lanes), lambda i, k=k: (0, 0, first // rows + i, k))
        )
    for table in tables:
        for piece in table:
            operands.append(piece)
            in_specs.append(whole(piece))
    kept = [k for k, array in enumerate(before) if array is not None]
    aliases = {len(operands) + n: k for n, k in enumerate(kept)}
    operands += [before[k] for k in kept]
    in_specs += [pl.BlockSpec(memory_space=pl.ANY)] * len(kept)
    kernel = functools.partial(
        spectral_kernel,
        pieces_in=len(pieces),
        pieces_out=pieces_out,
        pieces_wide=padded // lanes,
        sign=sign,
        extra=add is not None,
        carried=len(kept),
    )
    lead = (devices, planes_out, 2)
    return pl.pallas_call(
        kernel,
        grid=(count // rows,),
        in_specs=in_specs,
        out_specs=[exchange(planes_out, start) for start, _ in totals],
        out_shape=[jax.ShapeDtypeStruct((*lead, rows, width), F32) for _, rows in totals],
        input_output_aliases=aliases,
        scratch_shapes=[pltpu.VMEM((rows, 2 * domain, padded), BF16)] * 2
        + [pltpu.VMEM((rows * domain, 2 * padded), BF16)] * 2,
        compiler_params=params(),
        cost_estimate=cost(8 * count / part, spectrum),
    )(*operands)


def inverse_rows(got_refs, high, low):
    _, planes, _, _, width = got_refs[0].shape
    stacked = jnp.concatenate(
        [side_by_side([r[:, i].reshape(-1, width) for i in range(planes)]) for r in got_refs], 0
    )
    product = table_left(high, low, stacked)
    depth = product.shape[0] // 2
    return [
        [product[p * depth : (p + 1) * depth, i * width : (i + 1) * width] for i in range(planes)]
        for p in range(2)
    ]


def total_kernel(count, *refs):
    src_ref, inc_ref, high_ref, low_ref, *_ = refs[count:]
    scat_ref, sums_ref = refs[-2:]
    scat = inverse_rows(refs[:count], high_ref[...], low_ref[...])
    for i in range(src_ref.shape[1]):
        scat_real, scat_imag = scat[0][i], scat[1][i]
        scat_ref[0, i], scat_ref[1, i] = scat_real, scat_imag
        total_real, total_imag = inc_ref[0, i] + scat_real, inc_ref[1, i] + scat_imag
        src_real, src_imag = src_ref[0, i], src_ref[1, i]
        sums_ref[0, i] = src_real * total_real + src_imag * total_imag
        sums_ref[1, i] = src_imag * total_real - src_real * total_imag
        sums_ref[2, i] = total_real * total_real + total_imag * total_imag


def plane_spec(lead, step, depth, width, first):
    return pl.BlockSpec((lead, step, depth, width), lambda i: (0, first + i, 0, 0))


def step_of(planes, most=2):
    return next(step for step in (most, 2, 1) if planes % step == 0)


def total_call(gots, src, inc, table, piece, scat=None):
    devices, planes, _, _, width = gots[0].shape
    _, all_planes, depth, _ = src.shape
    step = step_of(planes)
    first = piece * planes // step
    high, low = table
    there = plane_spec(2, step, depth, width, first)
    operands = [*gots, src, inc, high, low]
    in_specs = [
        pl.BlockSpec((devices, step, 2, got.shape[3], width), lambda i: (0, i, 0, 0, 0)) for got in gots
    ] + [
        there,
        there,
        whole(high),
        whole(low),
    ]
    aliases = {}
    if scat is not None:
        aliases = {len(operands): 0}
        operands.append(scat)
        in_specs.append(pl.BlockSpec(memory_space=pl.ANY))
    return pl.pallas_call(
        functools.partial(total_kernel, len(gots)),
        grid=(planes // step,),
        in_specs=in_specs,
        out_specs=[there, plane_spec(3, step, depth, width, 0)],
        out_shape=[
            jax.ShapeDtypeStruct(src.shape, F32),
            jax.ShapeDtypeStruct((3, planes, depth, width), F32),
        ],
        input_output_aliases=aliases,
        compiler_params=params(),
        cost_estimate=cost(9, *gots),
    )(*operands)


def sums_here(own_ref, mine_ref, other_ref):
    half = (pl.program_id(0) * 2) // pl.num_programs(0)
    return jnp.where(half == own_ref[0, 0], mine_ref[...], other_ref[...])


def contrast_of(sums, con_ref, i):
    weight = sums[2, i] + tikhonov
    return tuple((sums[p, i] + tikhonov * con_ref[p, i]) / weight for p in range(2))


def norm_kernel(own_ref, mine_ref, other_ref, con_ref, power_ref, norm_ref):
    sums = sums_here(own_ref, mine_ref, other_ref)
    norm = jnp.zeros(norm_ref.shape, F32)
    for i in range(con_ref.shape[1]):
        chi_real, chi_imag = contrast_of(sums, con_ref, i)
        spread = (chi_real * chi_real + chi_imag * chi_imag) * power_ref[0, i]
        norm = norm + jnp.sum(spread.reshape((-1,) + norm.shape), 0)

    @pl.when(pl.program_id(0) == 0)
    def start():
        norm_ref[...] = norm

    @pl.when(pl.program_id(0) > 0)
    def add():
        norm_ref[...] += norm


def norm_call(sums, contrast, power, piece):
    mine, other, own = sums
    _, half_planes, depth, width = mine.shape
    step = step_of(half_planes, 4)
    first = piece * 2 * half_planes // step
    halved = pl.BlockSpec((3, step, depth, width), lambda i: (0, i % (half_planes // step), 0, 0))
    return pl.pallas_call(
        norm_kernel,
        grid=(2 * half_planes // step,),
        in_specs=[
            pl.BlockSpec(memory_space=pltpu.SMEM),
            halved,
            halved,
            plane_spec(2, step, depth, width, first),
            plane_spec(1, step, depth, width, first),
        ],
        out_specs=pl.BlockSpec((8, width), lambda i: (0, 0)),
        out_shape=jax.ShapeDtypeStruct((8, width), F32),
        compiler_params=params(),
        cost_estimate=cost(4, mine),
    )(own, mine, other, contrast, power)


def drive_kernel(count, own_ref, mine_ref, other_ref, con_ref, src_ref, inc_ref, scat_ref, high_ref, low_ref, *refs):
    *out_refs, chi_ref, base_ref = refs[-2 - count :]
    planes = src_ref.shape[1]
    sums_ref = sums_here(own_ref, mine_ref, other_ref)
    drive = [[], []]
    for i in range(planes):
        chi_real, chi_imag = contrast_of(sums_ref, con_ref, i)
        chi_ref[0, i], chi_ref[1, i] = chi_real, chi_imag
        total_real = inc_ref[0, i] + scat_ref[0, i]
        total_imag = inc_ref[1, i] + scat_ref[1, i]
        src_real, src_imag = src_ref[0, i], src_ref[1, i]
        res_real = chi_real * total_real - chi_imag * total_imag - src_real
        res_imag = chi_real * total_imag + chi_imag * total_real - src_imag
        base_ref[0, i] = src_real + step_length * res_real
        base_ref[1, i] = src_imag + step_length * res_imag
        drive[0].append(-(chi_real * res_real + chi_imag * res_imag))
        drive[1].append(chi_imag * res_real - chi_real * res_imag)
    forward_rows(drive, high_ref[...], low_ref[...], out_refs)


def drive_call(sums, contrast, src, inc, scat, table, devices, cuts, piece, before=()):
    mine, other, own = sums
    _, half_planes, depth, width = mine.shape
    planes = 2 * half_planes
    step = step_of(half_planes)
    first = piece * planes // step
    high, low = table
    there = plane_spec(2, step, depth, width, first)
    operands = [own, mine, other, contrast, src, inc, scat, high, low, *before]
    halved = pl.BlockSpec((3, step, depth, width), lambda i: (0, i % (half_planes // step), 0, 0))
    in_specs = [
        pl.BlockSpec(memory_space=pltpu.SMEM),
        halved,
        halved,
        there,
        there,
        there,
        there,
        whole(high),
        whole(low),
    ] + [pl.BlockSpec(memory_space=pl.ANY)] * len(before)
    return pl.pallas_call(
        functools.partial(drive_kernel, len(cuts)),
        grid=(planes // step,),
        in_specs=in_specs,
        out_specs=[
            pl.BlockSpec((devices, step, 2, cut, width), lambda i: (0, i, 0, 0, 0)) for cut in cuts
        ]
        + [there, there],
        out_shape=[jax.ShapeDtypeStruct((devices, planes, 2, cut, width), F32) for cut in cuts]
        + [jax.ShapeDtypeStruct(src.shape, F32)] * 2,
        input_output_aliases={9: len(cuts), 10: len(cuts) + 1} if before else {},
        compiler_params=params(),
        cost_estimate=cost(16, mine),
    )(*operands)


def last_kernel(*refs):
    *got_refs, base_ref, high_ref, low_ref, out_ref = refs
    back = inverse_rows(got_refs, high_ref[...], low_ref[...])
    for part in range(2):
        for i in range(base_ref.shape[1]):
            out_ref[part, i] = base_ref[part, i] + step_length * back[part][i]


def last_call(gots, base, table):
    _, planes, depth, width = base.shape
    step = step_of(planes, 8)
    high, low = table
    there = plane_spec(2, step, depth, width, 0)
    return pl.pallas_call(
        last_kernel,
        grid=(planes // step,),
        in_specs=[
            pl.BlockSpec((got.shape[0], step, 2, got.shape[3], width), lambda i: (0, i, 0, 0, 0))
            for got in gots
        ]
        + [there, whole(high), whole(low)],
        out_specs=there,
        out_shape=jax.ShapeDtypeStruct(base.shape, F32),
        compiler_params=params(),
        cost_estimate=cost(12, base),
    )(*gots, base, high, low)


def sample_kernel(index_ref, field_ref, out_ref):
    _, planes, depth, width = field_ref.shape
    count = out_ref.shape[0]
    rows = planes * depth
    field = jnp.concatenate([field_ref[p].reshape(rows, width) for p in range(2)], 1)
    at = lax.broadcasted_iota(jnp.int32, (count, rows), 1) + pl.program_id(0) * rows
    at = jnp.where(at == index_ref[...], 1.0, 0.0).astype(BF16)
    high, rest = split(field)
    low = field - high.astype(F32) - rest.astype(F32)
    got = mm(at, high) + (mm(at, rest) + mm(at, low.astype(BF16)))

    @pl.when(pl.program_id(0) == 0)
    def start():
        out_ref[...] = got

    @pl.when(pl.program_id(0) > 0)
    def add():
        out_ref[...] += got


def sample_call(index, field):
    _, planes, depth, width = field.shape
    count = index.shape[0]
    step = step_of(planes)
    return pl.pallas_call(
        sample_kernel,
        grid=(planes // step,),
        in_specs=[whole(index), plane_spec(2, step, depth, width, 0)],
        out_specs=pl.BlockSpec((count, 2 * width), lambda i: (0, 0)),
        out_shape=jax.ShapeDtypeStruct((count, 2 * width), F32),
        compiler_params=params(),
        cost_estimate=cost(16, field),
    )(index, field)


def placed_kernel(row_ref, column_ref, turned_ref, out_ref):
    rows, domain, _ = out_ref.shape
    count = row_ref.shape[1]
    width = out_ref.shape[2] // 2
    at_a = lax.broadcasted_iota(jnp.int32, (domain, count), 0) == row_ref[...]
    at_a = jnp.where(at_a, 1.0, 0.0).astype(BF16)
    at_c = lax.broadcasted_iota(jnp.int32, (width, count), 0) == column_ref[...]
    at_c = jnp.where(at_c, 1.0, 0.0)
    contract = (((1,), (1,)), ((), ()))
    for j in range(rows):
        field = jnp.concatenate([at_c * turned_ref[0, pl.ds(j, 1)], at_c * turned_ref[1, pl.ds(j, 1)]], 0)
        high, low = split(field)
        out_ref[j] = lax.dot_general(
            at_a, high, contract, preferred_element_type=F32
        ) + lax.dot_general(at_a, low, contract, preferred_element_type=F32)


def placed_call(row, column, turned, domain, width):
    _, part, count = turned.shape
    rows = ROWS if part % ROWS == 0 else part
    return pl.pallas_call(
        placed_kernel,
        grid=(part // rows,),
        in_specs=[
            whole(row),
            whole(column),
            pl.BlockSpec((2, rows, count), lambda i: (0, i, 0)),
        ],
        out_specs=pl.BlockSpec((rows, domain, 2 * width), lambda i: (i, 0, 0)),
        out_shape=jax.ShapeDtypeStruct((part, domain, 2 * width), F32),
        compiler_params=params(),
        cost_estimate=pl.CostEstimate(
            flops=12 * part * domain * 2 * width * count, bytes_accessed=0, transcendentals=0
        ),
    )(row, column, turned)


def flipped(value, axis, count, bits):
    return lax.ppermute(value, axis, [(i, i ^ bits) for i in range(count)])


def stages_of(count):
    stages, low, width = [], 1, 2
    while low < count:
        width = min(width, count // low)
        stages.append([k * low for k in range(1, width)])
        low, width = low * width, 4
    return stages


def sum_begun(value, axis, count):
    if count & (count - 1):
        return lax.psum(value, axis), []
    *stages, last = stages_of(count)
    for stage in stages:
        value = value + sum(flipped(value, axis, count, bits) for bits in stage)
    return value, [flipped(value, axis, count, bits) for bits in last]


def sum_halved(value, axis, count, beside=()):
    half = value.shape[1] // 2
    if count & (count - 1) or count < 2 or value.shape[1] % 2:
        value = lax.psum(value, axis)
        return (value[:, :half], value[:, half:], jnp.zeros((1, 1), jnp.int32)), beside
    me = lax.axis_index(axis) % 2
    mine = lax.dynamic_slice_in_dim(value, me * half, half, 1)
    other = lax.dynamic_slice_in_dim(value, (1 - me) * half, half, 1)
    mine = mine + flipped(other, axis, count, 1)
    low = 2
    while low < count:
        got, *beside = lax.optimization_barrier((flipped(mine, axis, count, low), *beside))
        mine = mine + got
        low *= 2
    return (mine, flipped(mine, axis, count, 1), me.astype(jnp.int32).reshape(1, 1)), beside


def shards(transmitters, devices, sources, contrast, spectrum, measured, receivers, positions):
    src = sources.reshape(sources.shape[1:])
    _, planes, depth, width = src.shape
    _, padded, part, _ = spectrum.shape
    domain = devices * planes
    halves = 2 if planes % 2 == 0 else 1
    place = lax.axis_index("gz")
    offset = place * planes

    natural = np.arange(domain)
    cut = split_order(devices, planes, halves)
    wide = np.arange(padded)
    if part % ROWS == 0 and part > ROWS:
        half = part // (2 * ROWS) * ROWS
        cuts_out, cuts_back = (part - half, half), (half, part - half)
    else:
        cuts_out = cuts_back = (part,)

    def forward_b(cuts):
        table = left_table(wide, np.arange(depth), padded, -1.0, 1.0)
        return two_parts(table[spread_order(devices, cuts)])

    def inverse_b(cuts):
        table = left_table(np.arange(depth), wide, padded, 1.0, padded)
        return two_parts(table[:, spread_order(devices, cuts)])

    forward_c = two_parts(right_table(np.arange(width), wide, padded, -1.0, 1.0))
    inverse_c = two_parts(right_table(wide, np.arange(width), padded, 1.0, padded))

    def along_a(order_in, order_out):
        return (
            forward_c,
            two_parts(left_table(wide, order_in, padded, -1.0, 1.0)),
            two_parts(left_table(order_out, wide, padded, 1.0, padded)),
            inverse_c,
        )

    def exchange(array):
        return lax.all_to_all(array, "gz", 0, 0)

    sent = first_call(src, forward_b(cuts_out), devices, cuts_out)
    gots_out = [exchange(sent[0])]

    shape = (planes, depth, width)
    first_axis = lax.broadcasted_iota(jnp.int32, shape, 0) + offset + depth // 4

    def radius_of(position):
        second = lax.broadcasted_iota(jnp.int32, shape, 1) - position[0]
        third = lax.broadcasted_iota(jnp.int32, shape, 2) - position[1]
        squared = first_axis * first_axis + second * second + third * third
        return jnp.sqrt(squared.astype(F32))

    radius = radius_of(positions[0])
    amplitude = reach_cells / (reach_cells + radius)
    angle = wave_number * radius
    inc = jnp.stack([amplitude * jnp.cos(angle), amplitude * jnp.sin(angle)])
    everywhere = lax.all_gather(positions, "tx", axis=0, tiled=True)
    power = jnp.zeros(shape, F32)
    for j in range(everywhere.shape[0]):
        level = reach_cells / (reach_cells + radius_of(everywhere[j]))
        power = power + level * level
    power = power[None]
    data_norm = lax.psum(jnp.sum(measured * measured), "tx")

    cell = receivers[0]
    row, rest = cell // (depth * width), cell % (depth * width)
    second, third = rest // width, rest % width
    rows_kb = place * part + lax.broadcasted_iota(jnp.int32, (part, cell.shape[0]), 0)
    turn = (rows_kb * second[None] % padded).astype(F32) * (2.0 * math.pi / padded)
    cos, sin = jnp.cos(turn), jnp.sin(turn)
    device_of, plane_of = row // planes, row % planes
    piece_planes = planes // halves
    row_place = (plane_of // piece_planes) * (devices * piece_planes) + device_of * piece_planes
    row_place = row_place + plane_of % piece_planes
    lane = lax.broadcasted_iota(jnp.int32, (cell.shape[0], width), 1) == third[:, None]

    if len(cuts_out) > 1:
        last, inc, power, data_norm, cos, sin = lax.optimization_barrier(
            (sent[1], inc, power, data_norm, cos, sin)
        )
        gots_out.append(exchange(last))

    tables, outs, first = along_a(natural, cut), (None,) * halves, 0
    gots = [[] for _ in range(halves)]
    for got, count in zip(gots_out, cuts_out):
        totals = [(0, count)] + [(first, part)] * (halves - 1)
        outs = spectral_call(
            [got], spectrum, tables, planes, 1.0, [0], (first, count), totals, before=(None, *outs[1:])
        )
        sent_now = outs[0]
        if gots[0]:
            sent_now, gots[0][-1] = lax.optimization_barrier((sent_now, gots[0][-1]))
        gots[0].append(exchange(sent_now))
        first += count
    for h in range(1, halves):
        gots[h].append(exchange(outs[h]))

    cuts_half = [(part,)] * (halves - 1) + [cuts_back]
    inverse_all = [inverse_b(cuts_out)] + [inverse_b((part,))] * (halves - 1)
    scat, summed, carried, sends, norms = None, None, (), [], []
    for h in range(halves):
        scat, sums = total_call(gots[h], src, inc, inverse_all[h], h, scat)
        if h < halves - 1:
            summed, _ = sum_halved(sums, "tx", transmitters)
        else:
            inside = (row >= offset) & (row < offset + planes)
            index = jnp.where(inside, (row - offset) * depth + second, -1)
            got = sample_call(index[:, None], scat)
            seen = [jnp.sum(jnp.where(lane, got[:, p * width : (p + 1) * width], 0.0), 1) for p in range(2)]
            seen = jnp.stack(seen)
            summed, (seen, *norms) = sum_halved(sums, "tx", transmitters, [seen, *norms])
        norms.append(norm_call(summed, contrast, power, h))
        if h == halves - 1:
            small = jnp.concatenate([seen.reshape(-1), sum(norms).reshape(-1)])
            small, arriving = sum_begun(small, "gz", devices)
        *send, chi, base = drive_call(
            summed, contrast, src, inc, scat, forward_b(cuts_half[h]), devices, cuts_half[h], h, carried
        )
        carried = (chi, base)
        if h < halves - 1:
            sends.append([exchange(send[0])])
    chi, base = carried

    going = sends[-1][-1] if sends else chi
    send[0], going, *arriving = lax.optimization_barrier((send[0], going, *arriving))
    if sends:
        sends[-1][-1] = going
    sends.append([exchange(send[0])])

    small = small + sum(arriving)
    seen, norm = small[: seen.size].reshape(seen.shape), small[seen.size :]
    misfit = measured[0] - seen
    turned = jnp.stack(
        [misfit[:1] * cos + misfit[1:] * sin, misfit[1:] * cos - misfit[:1] * sin]
    )
    add = placed_call(row_place[None], third[None], turned, domain, width)
    ratio = jnp.sum(norm).reshape(1, 1) / (data_norm + norm_floor)
    for later in send[1:]:
        later, sends[-1][-1], add = lax.optimization_barrier((later, sends[-1][-1], add))
        sends[-1].append(exchange(later))

    tables, gots, first = along_a(cut, natural), [], 0
    for q, count in enumerate(cuts_back):
        (out,) = spectral_call(
            [send[0] for send in sends[:-1]] + [sends[-1][q]],
            spectrum,
            tables,
            planes,
            -1.0,
            [first] * (halves - 1) + [0],
            (first, count),
            [(0, count)],
            add,
            ratio,
        )
        gots.append(exchange(out))
        first += count
    new = last_call(gots, base, inverse_b(cuts_back))
    return new[None], chi


def solution(mesh):
    in_specs = (
        P("tx", None, "gz", None, None),
        P(None, "gz", None, None),
        P(None, None, "gz", None),
        P("tx", None, None),
        P("tx", None),
        P("tx", None),
    )
    out_specs = (P("tx", None, "gz", None, None), P(None, "gz", None, None))
    body = functools.partial(shards, mesh.shape["tx"], mesh.shape["gz"])
    return jax.shard_map(body, mesh=mesh, in_specs=in_specs, out_specs=out_specs, check_vma=False)
```

```python
import functools
import math

import jax
import jax.numpy as jnp
import numpy as np
from jax import lax
from jax.experimental import pallas as pl
from jax.experimental.pallas import tpu as pltpu
from jax.sharding import PartitionSpec as P

wave_number = 2.0 * math.pi / 12.0
reach_cells = 16.0
tikhonov = 1.0
step_length = 0.5
norm_floor = 1e-06

ROWS = 8
LANES = 128
UNROLL = 4
VMEM_LIMIT = 63 * 1024 * 1024
F32 = jnp.float32
BF16 = jnp.bfloat16


def two_parts(table):
    table = np.asarray(table, np.float64)
    high = table.astype(np.float32).astype(jnp.bfloat16)
    low = (table - high.astype(np.float64)).astype(np.float32).astype(jnp.bfloat16)
    return np.asarray(high), np.asarray(low)


def phases(rows, columns, period, sign, divisor):
    angle = (np.outer(rows, columns) % period) * (2.0 * np.pi / period)
    return np.cos(angle) / divisor, sign * np.sin(angle) / divisor


def left_table(rows, columns, period, sign, divisor):
    cos, sin = phases(rows, columns, period, sign, divisor)
    return np.concatenate([np.concatenate([cos, -sin], 1), np.concatenate([sin, cos], 1)], 0)


def right_table(rows, columns, period, sign, divisor):
    return left_table(columns, rows, period, sign, divisor).T


def spread_order(devices, cuts):
    order = np.arange(2 * devices * sum(cuts)).reshape(2, devices, sum(cuts))
    ends = np.cumsum(cuts)
    pieces = [order[:, :, end - cut : end] for cut, end in zip(cuts, ends)]
    return np.concatenate([piece.transpose(1, 0, 2).reshape(-1) for piece in pieces])


def split_order(devices, planes, pieces):
    order = np.arange(devices * planes).reshape(devices, pieces, planes // pieces)
    return order.transpose(1, 0, 2).reshape(-1)


def split(value):
    high = value.astype(BF16)
    return high, (value - high.astype(F32)).astype(BF16)


def mm(left, right):
    return jnp.dot(left, right, preferred_element_type=F32)


def three(left_high, left_low, right_high, right_low):
    return mm(left_high, right_high) + (mm(left_high, right_low) + mm(left_low, right_high))


def table_left(high, low, value):
    return three(high, low, *split(value))


def table_right(value, high, low):
    return three(*split(value), high, low)


def whole(array):
    return pl.BlockSpec(array.shape, lambda *i: (0,) * array.ndim)


def params():
    return pltpu.CompilerParams(vmem_limit_bytes=VMEM_LIMIT)


def cost(factor, *arrays):
    size = sum(4 * math.prod(array.shape) for array in arrays)
    return pl.CostEstimate(flops=0, bytes_accessed=int(factor * size), transcendentals=0)


def side_by_side(planes):
    return jnp.concatenate(planes, 1) if len(planes) > 1 else planes[0]


def forward_rows(field, high, low, out_refs):
    stacked = jnp.concatenate([side_by_side(field[0]), side_by_side(field[1])], 0)
    product = table_left(high, low, stacked)
    first = 0
    for out_ref in out_refs:
        devices, planes, _, part, width = out_ref.shape
        count = devices * 2 * part
        for i in range(planes):
            piece = product[first : first + count, i * width : (i + 1) * width]
            out_ref[:, i] = piece.reshape(devices, 2, part, width)
        first += count


def first_kernel(src_ref, high_ref, low_ref, *out_refs):
    planes = src_ref.shape[1]
    field = [[src_ref[part, i] for i in range(planes)] for part in range(2)]
    forward_rows(field, high_ref[...], low_ref[...], out_refs)


def first_call(src, table, devices, cuts):
    _, planes, depth, width = src.shape
    step = 2 if planes % 2 == 0 else 1
    high, low = table
    return pl.pallas_call(
        first_kernel,
        grid=(planes // step,),
        in_specs=[
            pl.BlockSpec((2, step, depth, width), lambda i: (0, i, 0, 0)),
            whole(high),
            whole(low),
        ],
        out_specs=[
            pl.BlockSpec((devices, step, 2, cut, width), lambda i: (0, i, 0, 0, 0)) for cut in cuts
        ],
        out_shape=[jax.ShapeDtypeStruct((devices, planes, 2, cut, width), F32) for cut in cuts],
        compiler_params=params(),
        cost_estimate=cost(12, src),
    )(src, high, low)


def spectral_kernel(*refs, pieces_in, pieces_out, pieces_wide, sign, extra, carried):
    refs = list(refs)
    ins = [refs.pop(0) for _ in range(pieces_in)]
    if extra:
        add_ref, ratio_ref = refs.pop(0), refs.pop(0)
    specs = [refs.pop(0) for _ in range(pieces_wide)]
    tch, tcl, tah, tal, tiah, tial, tich, ticl = (refs.pop(0) for _ in range(8))
    refs = refs[carried:]
    outs = [refs.pop(0) for _ in range(pieces_out)]
    mid_high, mid_low, end_high, end_low = refs
    _, padded, rows, lanes = specs[0].shape
    domain = tial.shape[0] // 2
    width = ins[0].shape[-1]
    flat_in = [r.reshape(-1, width) for r in ins]
    flat_out = [r.reshape(-1, width) for r in outs]
    flat_spec = [r.reshape(2 * padded * rows, lanes) for r in specs]
    count_in, count_out = domain // pieces_in, domain // pieces_out

    def planes_in(j):
        parts = []
        for part in range(2):
            got = [r[pl.ds(part * rows + j, count_in, stride=2 * rows), :] for r in flat_in]
            parts.append(jnp.concatenate(got, 0) if len(got) > 1 else got[0])
        plane = jnp.concatenate(parts, 1)
        return plane + ratio_ref[0, 0] * add_ref[j] if extra else plane

    along_c = table_right(jnp.concatenate([planes_in(j) for j in range(rows)], 0), tch[...], tcl[...])
    for j in range(rows):
        piece = along_c[j * domain : (j + 1) * domain]
        high, low = split(piece)
        for part in range(2):
            lanes_of = slice(part * padded, (part + 1) * padded)
            mid_high[j, part * domain : (part + 1) * domain] = high[:, lanes_of]
            mid_low[j, part * domain : (part + 1) * domain] = low[:, lanes_of]

    def body(j, carry):
        chunk = padded // 2
        back = None
        for c in range(2):
            picked = [slice(p * padded + c * chunk, p * padded + (c + 1) * chunk) for p in range(2)]
            high = jnp.concatenate([tah[r, :] for r in picked], 0)
            low = jnp.concatenate([tal[r, :] for r in picked], 0)
            full = three(high, low, mid_high[j], mid_low[j])
            real, imag = full[:chunk], full[chunk:]
            spec_real, spec_imag = (
                side_by_side([r[pl.ds(p.start * rows + j, chunk, stride=rows), :] for r in flat_spec])
                for p in picked
            )
            if sign > 0:
                new_real = real * spec_real - imag * spec_imag
                new_imag = real * spec_imag + imag * spec_real
            else:
                new_real = real * spec_real + imag * spec_imag
                new_imag = imag * spec_real - real * spec_imag
            high = jnp.concatenate([tiah[:, r] for r in picked], 1)
            low = jnp.concatenate([tial[:, r] for r in picked], 1)
            term = table_left(high, low, jnp.concatenate([new_real, new_imag], 0))
            back = term if back is None else back + term
        high, low = split(jnp.concatenate([back[:domain], back[domain:]], 1))
        start = pl.multiple_of(j * domain, domain)
        end_high[pl.ds(start, domain), :] = high
        end_low[pl.ds(start, domain), :] = low
        return carry

    lax.fori_loop(0, rows, body, 0, unroll=UNROLL)
    result = three(end_high[...], end_low[...], tich[...], ticl[...])
    for j in range(rows):
        for part in range(2):
            for h, r in enumerate(flat_out):
                first = j * domain + h * count_out
                r[pl.ds(part * rows + j, count_out, stride=2 * rows), :] = result[
                    first : first + count_out, part * width : (part + 1) * width
                ]


def spectral_call(
    pieces, spectrum, tables, planes, sign, rows_in, rows_of, totals, add=None, ratio=None, before=()
):
    devices, planes_in, _, _, width = pieces[0].shape
    _, padded, part, _ = spectrum.shape
    pieces_out = len(totals)
    planes_out = planes // pieces_out
    first, count = rows_of
    rows = ROWS if count % ROWS == 0 else count
    domain = devices * planes

    def exchange(planes_here, start):
        return pl.BlockSpec(
            (devices, planes_here, 2, rows, width), lambda i: (0, 0, 0, start // rows + i, 0)
        )

    operands = list(pieces)
    in_specs = [exchange(planes_in, start) for start in rows_in]
    if add is not None:
        operands += [add, ratio]
        in_specs += [
            pl.BlockSpec((rows, domain, 2 * width), lambda i: (first // rows + i, 0, 0)),
            pl.BlockSpec(memory_space=pltpu.SMEM),
        ]
    lanes = LANES if padded % LANES == 0 else padded
    for k in range(padded // lanes):
        operands.append(spectrum)
        in_specs.append(
            pl.BlockSpec((2, padded, rows, lanes), lambda i, k=k: (0, 0, first // rows + i, k))
        )
    for table in tables:
        for piece in table:
            operands.append(piece)
            in_specs.append(whole(piece))
    kept = [k for k, array in enumerate(before) if array is not None]
    aliases = {len(operands) + n: k for n, k in enumerate(kept)}
    operands += [before[k] for k in kept]
    in_specs += [pl.BlockSpec(memory_space=pl.ANY)] * len(kept)
    kernel = functools.partial(
        spectral_kernel,
        pieces_in=len(pieces),
        pieces_out=pieces_out,
        pieces_wide=padded // lanes,
        sign=sign,
        extra=add is not None,
        carried=len(kept),
    )
    lead = (devices, planes_out, 2)
    return pl.pallas_call(
        kernel,
        grid=(count // rows,),
        in_specs=in_specs,
        out_specs=[exchange(planes_out, start) for start, _ in totals],
        out_shape=[jax.ShapeDtypeStruct((*lead, rows, width), F32) for _, rows in totals],
        input_output_aliases=aliases,
        scratch_shapes=[pltpu.VMEM((rows, 2 * domain, padded), BF16)] * 2
        + [pltpu.VMEM((rows * domain, 2 * padded), BF16)] * 2,
        compiler_params=params(),
        cost_estimate=cost(8 * count / part, spectrum),
    )(*operands)


def inverse_rows(got_refs, high, low):
    _, planes, _, _, width = got_refs[0].shape
    stacked = jnp.concatenate(
        [side_by_side([r[:, i].reshape(-1, width) for i in range(planes)]) for r in got_refs], 0
    )
    product = table_left(high, low, stacked)
    depth = product.shape[0] // 2
    return [
        [product[p * depth : (p + 1) * depth, i * width : (i + 1) * width] for i in range(planes)]
        for p in range(2)
    ]


def total_kernel(count, *refs):
    src_ref, inc_ref, high_ref, low_ref, *_ = refs[count:]
    scat_ref, sums_ref = refs[-2:]
    scat = inverse_rows(refs[:count], high_ref[...], low_ref[...])
    for i in range(src_ref.shape[1]):
        scat_real, scat_imag = scat[0][i], scat[1][i]
        scat_ref[0, i], scat_ref[1, i] = scat_real, scat_imag
        total_real, total_imag = inc_ref[0, i] + scat_real, inc_ref[1, i] + scat_imag
        src_real, src_imag = src_ref[0, i], src_ref[1, i]
        sums_ref[0, i] = src_real * total_real + src_imag * total_imag
        sums_ref[1, i] = src_imag * total_real - src_real * total_imag
        sums_ref[2, i] = total_real * total_real + total_imag * total_imag


def plane_spec(lead, step, depth, width, first):
    return pl.BlockSpec((lead, step, depth, width), lambda i: (0, first + i, 0, 0))


def step_of(planes, most=2):
    return next(step for step in (most, 2, 1) if planes % step == 0)


def total_call(gots, src, inc, table, piece, scat=None):
    devices, planes, _, _, width = gots[0].shape
    _, all_planes, depth, _ = src.shape
    step = step_of(planes, 4)
    first = piece * planes // step
    high, low = table
    there = plane_spec(2, step, depth, width, first)
    operands = [*gots, src, inc, high, low]
    in_specs = [
        pl.BlockSpec((devices, step, 2, got.shape[3], width), lambda i: (0, i, 0, 0, 0)) for got in gots
    ] + [
        there,
        there,
        whole(high),
        whole(low),
    ]
    aliases = {}
    if scat is not None:
        aliases = {len(operands): 0}
        operands.append(scat)
        in_specs.append(pl.BlockSpec(memory_space=pl.ANY))
    return pl.pallas_call(
        functools.partial(total_kernel, len(gots)),
        grid=(planes // step,),
        in_specs=in_specs,
        out_specs=[there, plane_spec(3, step, depth, width, 0)],
        out_shape=[
            jax.ShapeDtypeStruct(src.shape, F32),
            jax.ShapeDtypeStruct((3, planes, depth, width), F32),
        ],
        input_output_aliases=aliases,
        compiler_params=params(),
        cost_estimate=cost(9, *gots),
    )(*operands)


def sums_here(own_ref, mine_ref, other_ref):
    half = (pl.program_id(0) * 2) // pl.num_programs(0)
    return jnp.where(half == own_ref[0, 0], mine_ref[...], other_ref[...])


def contrast_of(sums, con_ref, i):
    weight = sums[2, i] + tikhonov
    return tuple((sums[p, i] + tikhonov * con_ref[p, i]) / weight for p in range(2))


def norm_kernel(own_ref, mine_ref, other_ref, con_ref, power_ref, norm_ref):
    sums = sums_here(own_ref, mine_ref, other_ref)
    norm = jnp.zeros(norm_ref.shape, F32)
    for i in range(con_ref.shape[1]):
        chi_real, chi_imag = contrast_of(sums, con_ref, i)
        spread = (chi_real * chi_real + chi_imag * chi_imag) * power_ref[0, i]
        norm = norm + jnp.sum(spread.reshape((-1,) + norm.shape), 0)

    @pl.when(pl.program_id(0) == 0)
    def start():
        norm_ref[...] = norm

    @pl.when(pl.program_id(0) > 0)
    def add():
        norm_ref[...] += norm


def norm_call(sums, contrast, power, piece):
    mine, other, own = sums
    _, half_planes, depth, width = mine.shape
    step = step_of(half_planes, 4)
    first = piece * 2 * half_planes // step
    halved = pl.BlockSpec((3, step, depth, width), lambda i: (0, i % (half_planes // step), 0, 0))
    return pl.pallas_call(
        norm_kernel,
        grid=(2 * half_planes // step,),
        in_specs=[
            pl.BlockSpec(memory_space=pltpu.SMEM),
            halved,
            halved,
            plane_spec(2, step, depth, width, first),
            plane_spec(1, step, depth, width, first),
        ],
        out_specs=pl.BlockSpec((8, width), lambda i: (0, 0)),
        out_shape=jax.ShapeDtypeStruct((8, width), F32),
        compiler_params=params(),
        cost_estimate=cost(4, mine),
    )(own, mine, other, contrast, power)


def drive_kernel(count, own_ref, mine_ref, other_ref, con_ref, src_ref, inc_ref, scat_ref, high_ref, low_ref, *refs):
    *out_refs, chi_ref, base_ref = refs[-2 - count :]
    planes = src_ref.shape[1]
    sums_ref = sums_here(own_ref, mine_ref, other_ref)
    drive = [[], []]
    for i in range(planes):
        chi_real, chi_imag = contrast_of(sums_ref, con_ref, i)
        chi_ref[0, i], chi_ref[1, i] = chi_real, chi_imag
        total_real = inc_ref[0, i] + scat_ref[0, i]
        total_imag = inc_ref[1, i] + scat_ref[1, i]
        src_real, src_imag = src_ref[0, i], src_ref[1, i]
        res_real = chi_real * total_real - chi_imag * total_imag - src_real
        res_imag = chi_real * total_imag + chi_imag * total_real - src_imag
        base_ref[0, i] = src_real + step_length * res_real
        base_ref[1, i] = src_imag + step_length * res_imag
        drive[0].append(-(chi_real * res_real + chi_imag * res_imag))
        drive[1].append(chi_imag * res_real - chi_real * res_imag)
    forward_rows(drive, high_ref[...], low_ref[...], out_refs)


def drive_call(sums, contrast, src, inc, scat, table, devices, cuts, piece, before=()):
    mine, other, own = sums
    _, half_planes, depth, width = mine.shape
    planes = 2 * half_planes
    step = step_of(half_planes, 4)
    first = piece * planes // step
    high, low = table
    there = plane_spec(2, step, depth, width, first)
    operands = [own, mine, other, contrast, src, inc, scat, high, low, *before]
    halved = pl.BlockSpec((3, step, depth, width), lambda i: (0, i % (half_planes // step), 0, 0))
    in_specs = [
        pl.BlockSpec(memory_space=pltpu.SMEM),
        halved,
        halved,
        there,
        there,
        there,
        there,
        whole(high),
        whole(low),
    ] + [pl.BlockSpec(memory_space=pl.ANY)] * len(before)
    return pl.pallas_call(
        functools.partial(drive_kernel, len(cuts)),
        grid=(planes // step,),
        in_specs=in_specs,
        out_specs=[
            pl.BlockSpec((devices, step, 2, cut, width), lambda i: (0, i, 0, 0, 0)) for cut in cuts
        ]
        + [there, there],
        out_shape=[jax.ShapeDtypeStruct((devices, planes, 2, cut, width), F32) for cut in cuts]
        + [jax.ShapeDtypeStruct(src.shape, F32)] * 2,
        input_output_aliases={9: len(cuts), 10: len(cuts) + 1} if before else {},
        compiler_params=params(),
        cost_estimate=cost(16, mine),
    )(*operands)


def last_kernel(*refs):
    *got_refs, base_ref, high_ref, low_ref, out_ref = refs
    back = inverse_rows(got_refs, high_ref[...], low_ref[...])
    for part in range(2):
        for i in range(base_ref.shape[1]):
            out_ref[part, i] = base_ref[part, i] + step_length * back[part][i]


def last_call(gots, base, table):
    _, planes, depth, width = base.shape
    step = step_of(planes, 8)
    high, low = table
    there = plane_spec(2, step, depth, width, 0)
    return pl.pallas_call(
        last_kernel,
        grid=(planes // step,),
        in_specs=[
            pl.BlockSpec((got.shape[0], step, 2, got.shape[3], width), lambda i: (0, i, 0, 0, 0))
            for got in gots
        ]
        + [there, whole(high), whole(low)],
        out_specs=there,
        out_shape=jax.ShapeDtypeStruct(base.shape, F32),
        compiler_params=params(),
        cost_estimate=cost(12, base),
    )(*gots, base, high, low)


def sample_kernel(index_ref, field_ref, out_ref):
    _, planes, depth, width = field_ref.shape
    count = out_ref.shape[0]
    rows = planes * depth
    field = jnp.concatenate([field_ref[p].reshape(rows, width) for p in range(2)], 1)
    at = lax.broadcasted_iota(jnp.int32, (count, rows), 1) + pl.program_id(0) * rows
    at = jnp.where(at == index_ref[...], 1.0, 0.0).astype(BF16)
    high, rest = split(field)
    low = field - high.astype(F32) - rest.astype(F32)
    got = mm(at, high) + (mm(at, rest) + mm(at, low.astype(BF16)))

    @pl.when(pl.program_id(0) == 0)
    def start():
        out_ref[...] = got

    @pl.when(pl.program_id(0) > 0)
    def add():
        out_ref[...] += got


def sample_call(index, field):
    _, planes, depth, width = field.shape
    count = index.shape[0]
    step = step_of(planes)
    return pl.pallas_call(
        sample_kernel,
        grid=(planes // step,),
        in_specs=[whole(index), plane_spec(2, step, depth, width, 0)],
        out_specs=pl.BlockSpec((count, 2 * width), lambda i: (0, 0)),
        out_shape=jax.ShapeDtypeStruct((count, 2 * width), F32),
        compiler_params=params(),
        cost_estimate=cost(16, field),
    )(index, field)


def placed_kernel(row_ref, column_ref, turned_ref, out_ref):
    rows, domain, _ = out_ref.shape
    count = row_ref.shape[1]
    width = out_ref.shape[2] // 2
    at_a = lax.broadcasted_iota(jnp.int32, (domain, count), 0) == row_ref[...]
    at_a = jnp.where(at_a, 1.0, 0.0).astype(BF16)
    at_c = lax.broadcasted_iota(jnp.int32, (width, count), 0) == column_ref[...]
    at_c = jnp.where(at_c, 1.0, 0.0)
    contract = (((1,), (1,)), ((), ()))
    for j in range(rows):
        field = jnp.concatenate([at_c * turned_ref[0, pl.ds(j, 1)], at_c * turned_ref[1, pl.ds(j, 1)]], 0)
        high, low = split(field)
        out_ref[j] = lax.dot_general(
            at_a, high, contract, preferred_element_type=F32
        ) + lax.dot_general(at_a, low, contract, preferred_element_type=F32)


def placed_call(row, column, turned, domain, width):
    _, part, count = turned.shape
    rows = ROWS if part % ROWS == 0 else part
    return pl.pallas_call(
        placed_kernel,
        grid=(part // rows,),
        in_specs=[
            whole(row),
            whole(column),
            pl.BlockSpec((2, rows, count), lambda i: (0, i, 0)),
        ],
        out_specs=pl.BlockSpec((rows, domain, 2 * width), lambda i: (i, 0, 0)),
        out_shape=jax.ShapeDtypeStruct((part, domain, 2 * width), F32),
        compiler_params=params(),
        cost_estimate=pl.CostEstimate(
            flops=12 * part * domain * 2 * width * count, bytes_accessed=0, transcendentals=0
        ),
    )(row, column, turned)


def flipped(value, axis, count, bits):
    return lax.ppermute(value, axis, [(i, i ^ bits) for i in range(count)])


def stages_of(count):
    stages, low, width = [], 1, 2
    while low < count:
        width = min(width, count // low)
        stages.append([k * low for k in range(1, width)])
        low, width = low * width, 4
    return stages


def sum_begun(value, axis, count):
    if count & (count - 1):
        return lax.psum(value, axis), []
    *stages, last = stages_of(count)
    for stage in stages:
        value = value + sum(flipped(value, axis, count, bits) for bits in stage)
    return value, [flipped(value, axis, count, bits) for bits in last]


def sum_halved(value, axis, count, beside=()):
    half = value.shape[1] // 2
    if count & (count - 1) or count < 2 or value.shape[1] % 2:
        value = lax.psum(value, axis)
        return (value[:, :half], value[:, half:], jnp.zeros((1, 1), jnp.int32)), beside
    me = lax.axis_index(axis) % 2
    mine = lax.dynamic_slice_in_dim(value, me * half, half, 1)
    other = lax.dynamic_slice_in_dim(value, (1 - me) * half, half, 1)
    mine = mine + flipped(other, axis, count, 1)
    low = 2
    while low < count:
        got, *beside = lax.optimization_barrier((flipped(mine, axis, count, low), *beside))
        mine = mine + got
        low *= 2
    return (mine, flipped(mine, axis, count, 1), me.astype(jnp.int32).reshape(1, 1)), beside


def shards(transmitters, devices, sources, contrast, spectrum, measured, receivers, positions):
    src = sources.reshape(sources.shape[1:])
    _, planes, depth, width = src.shape
    _, padded, part, _ = spectrum.shape
    domain = devices * planes
    halves = 2 if planes % 2 == 0 else 1
    place = lax.axis_index("gz")
    offset = place * planes

    natural = np.arange(domain)
    cut = split_order(devices, planes, halves)
    wide = np.arange(padded)
    if part % ROWS == 0 and part > ROWS:
        half = part // (2 * ROWS) * ROWS
        cuts_out, cuts_back = (part - half, half), (half, part - half)
    else:
        cuts_out = cuts_back = (part,)

    def forward_b(cuts):
        table = left_table(wide, np.arange(depth), padded, -1.0, 1.0)
        return two_parts(table[spread_order(devices, cuts)])

    def inverse_b(cuts):
        table = left_table(np.arange(depth), wide, padded, 1.0, padded)
        return two_parts(table[:, spread_order(devices, cuts)])

    forward_c = two_parts(right_table(np.arange(width), wide, padded, -1.0, 1.0))
    inverse_c = two_parts(right_table(wide, np.arange(width), padded, 1.0, padded))

    def along_a(order_in, order_out):
        return (
            forward_c,
            two_parts(left_table(wide, order_in, padded, -1.0, 1.0)),
            two_parts(left_table(order_out, wide, padded, 1.0, padded)),
            inverse_c,
        )

    def exchange(array):
        return lax.all_to_all(array, "gz", 0, 0)

    sent = first_call(src, forward_b(cuts_out), devices, cuts_out)
    gots_out = [exchange(sent[0])]

    shape = (planes, depth, width)
    first_axis = lax.broadcasted_iota(jnp.int32, shape, 0) + offset + depth // 4

    def radius_of(position):
        second = lax.broadcasted_iota(jnp.int32, shape, 1) - position[0]
        third = lax.broadcasted_iota(jnp.int32, shape, 2) - position[1]
        squared = first_axis * first_axis + second * second + third * third
        return jnp.sqrt(squared.astype(F32))

    radius = radius_of(positions[0])
    amplitude = reach_cells / (reach_cells + radius)
    angle = wave_number * radius
    inc = jnp.stack([amplitude * jnp.cos(angle), amplitude * jnp.sin(angle)])
    everywhere = lax.all_gather(positions, "tx", axis=0, tiled=True)
    power = jnp.zeros(shape, F32)
    for j in range(everywhere.shape[0]):
        level = reach_cells / (reach_cells + radius_of(everywhere[j]))
        power = power + level * level
    power = power[None]
    data_norm = lax.psum(jnp.sum(measured * measured), "tx")

    cell = receivers[0]
    row, rest = cell // (depth * width), cell % (depth * width)
    second, third = rest // width, rest % width
    rows_kb = place * part + lax.broadcasted_iota(jnp.int32, (part, cell.shape[0]), 0)
    turn = (rows_kb * second[None] % padded).astype(F32) * (2.0 * math.pi / padded)
    cos, sin = jnp.cos(turn), jnp.sin(turn)
    device_of, plane_of = row // planes, row % planes
    piece_planes = planes // halves
    row_place = (plane_of // piece_planes) * (devices * piece_planes) + device_of * piece_planes
    row_place = row_place + plane_of % piece_planes
    lane = lax.broadcasted_iota(jnp.int32, (cell.shape[0], width), 1) == third[:, None]

    if len(cuts_out) > 1:
        last, inc, power, data_norm, cos, sin = lax.optimization_barrier(
            (sent[1], inc, power, data_norm, cos, sin)
        )
        gots_out.append(exchange(last))

    tables, outs, first = along_a(natural, cut), (None,) * halves, 0
    gots = [[] for _ in range(halves)]
    for got, count in zip(gots_out, cuts_out):
        totals = [(0, count)] + [(first, part)] * (halves - 1)
        outs = spectral_call(
            [got], spectrum, tables, planes, 1.0, [0], (first, count), totals, before=(None, *outs[1:])
        )
        sent_now = outs[0]
        if gots[0]:
            sent_now, gots[0][-1] = lax.optimization_barrier((sent_now, gots[0][-1]))
        gots[0].append(exchange(sent_now))
        first += count
    for h in range(1, halves):
        gots[h].append(exchange(outs[h]))

    cuts_half = [(part,)] * (halves - 1) + [cuts_back]
    inverse_all = [inverse_b(cuts_out)] + [inverse_b((part,))] * (halves - 1)
    scat, summed, carried, sends, norms = None, None, (), [], []
    for h in range(halves):
        scat, sums = total_call(gots[h], src, inc, inverse_all[h], h, scat)
        if h < halves - 1:
            summed, _ = sum_halved(sums, "tx", transmitters)
        else:
            inside = (row >= offset) & (row < offset + planes)
            index = jnp.where(inside, (row - offset) * depth + second, -1)
            got = sample_call(index[:, None], scat)
            seen = [jnp.sum(jnp.where(lane, got[:, p * width : (p + 1) * width], 0.0), 1) for p in range(2)]
            seen = jnp.stack(seen)
            summed, (seen, *norms) = sum_halved(sums, "tx", transmitters, [seen, *norms])
        norms.append(norm_call(summed, contrast, power, h))
        if h == halves - 1:
            small = jnp.concatenate([seen.reshape(-1), sum(norms).reshape(-1)])
            small, arriving = sum_begun(small, "gz", devices)
        *send, chi, base = drive_call(
            summed, contrast, src, inc, scat, forward_b(cuts_half[h]), devices, cuts_half[h], h, carried
        )
        carried = (chi, base)
        if h < halves - 1:
            sends.append([exchange(send[0])])
    chi, base = carried

    going = sends[-1][-1] if sends else chi
    send[0], going, *arriving = lax.optimization_barrier((send[0], going, *arriving))
    if sends:
        sends[-1][-1] = going
    sends.append([exchange(send[0])])

    small = small + sum(arriving)
    seen, norm = small[: seen.size].reshape(seen.shape), small[seen.size :]
    misfit = measured[0] - seen
    turned = jnp.stack(
        [misfit[:1] * cos + misfit[1:] * sin, misfit[1:] * cos - misfit[:1] * sin]
    )
    add = placed_call(row_place[None], third[None], turned, domain, width)
    ratio = jnp.sum(norm).reshape(1, 1) / (data_norm + norm_floor)
    for later in send[1:]:
        later, sends[-1][-1], add = lax.optimization_barrier((later, sends[-1][-1], add))
        sends[-1].append(exchange(later))

    tables, gots, first = along_a(cut, natural), [], 0
    for q, count in enumerate(cuts_back):
        (out,) = spectral_call(
            [send[0] for send in sends[:-1]] + [sends[-1][q]],
            spectrum,
            tables,
            planes,
            -1.0,
            [first] * (halves - 1) + [0],
            (first, count),
            [(0, count)],
            add,
            ratio,
        )
        gots.append(exchange(out))
        first += count
    new = last_call(gots, base, inverse_b(cuts_back))
    return new[None], chi


def solution(mesh):
    in_specs = (
        P("tx", None, "gz", None, None),
        P(None, "gz", None, None),
        P(None, None, "gz", None),
        P("tx", None, None),
        P("tx", None),
        P("tx", None),
    )
    out_specs = (P("tx", None, "gz", None, None), P(None, "gz", None, None))
    body = functools.partial(shards, mesh.shape["tx"], mesh.shape["gz"])
    return jax.shard_map(body, mesh=mesh, in_specs=in_specs, out_specs=out_specs, check_vma=False)
```
